256 devices in a mesh: ctx: 32 (over z, y), head: 8 (over x, core).
Axes of the slice: x: 4, y: 4, z: 8, core: 2. Of those that a mesh axis runs over, the one named last changes fastest.
Arguments:
- residual: bfloat16 [8192, 1024], P(('ctx', 'head')), may hold values from -6 to 6
- input_gain: float32 [2, 1024], replicated, may hold values from 0.25 to 1.75
- project_in: bfloat16 [2, 3, 1024, 1024], P(None, None, None, 'head'), may hold values from -0.1875 to 0.1875
- output_gain: float32 [2, 1024], P(None, 'head'), may hold values from 0.25 to 1.75
- project_out: bfloat16 [2, 1024, 1024], P(None, 'head'), may hold values from -0.1875 to 0.1875
Outputs:
- result_rows: bfloat16 [8192, 1024], P(('ctx', 'head'))
The draws below stay inside these ranges and needn't reach their ends.
All inputs are finite; a program needn't handle non-finite values.
Results may differ from the reference program's by a relative error of at most 0.012.
Values may be sent and summed in bfloat16 or wider, within the bound.
A program may use at most 128 MiB of HBM per device.

```python
import jax
import jax.numpy as jnp
import numpy as np
from jax import lax

D = 1024
HEADS = 16
HD = 64
LAYERS = 2
CTX_TOK = 256
FEAT = 2080
TOKENS = 8192
N_CTX = 32


def shard_levels(rng, shape, pieces, least, largest):
    level, own = 1.0, jax.random.fold_in(rng, 6)
    for position, parts in pieces:
        heights = jnp.exp(jax.random.uniform(jax.random.fold_in(own, position), (parts,), jnp.float32, least / len(pieces), largest / len(pieces)))
        level = level * jnp.repeat(heights, shape[position] // parts).reshape([-1 if axis == position else 1 for axis in range(len(shape))])
    return level


def bell_draw(own_key, shape, scale, reach, shards=(), held_as=jnp.bfloat16):
    result = scale * jax.random.normal(own_key, shape, jnp.float32)
    if shards:
        result = result * shard_levels(own_key, shape, shards, -0.22, 0.18)
    return jnp.clip(result, -reach, reach).astype(held_as)


def setup_inputs(seed: int = 0) -> dict:
    key_of = jax.random.split(jax.random.key(seed), 6)
    return {
        "residual": bell_draw(key_of[0], (TOKENS, D), 1.0, 6.0, ((0, 256),)),
        "input_gain": jnp.clip(1.0 + 0.15 * jax.random.normal(key_of[1], (LAYERS, D), jnp.float32), 0.25, 1.75),
        "project_in": bell_draw(key_of[2], (LAYERS, 3, D, HEADS * HD), D ** -0.5, 0.1875, ((3, 8),)),
        "output_gain": jnp.clip(1.0 + 0.15 * jax.random.normal(key_of[3], (LAYERS, HEADS * HD), jnp.float32), 0.25, 1.75),
        "project_out": bell_draw(key_of[4], (LAYERS, HEADS * HD, D), (HEADS * HD) ** -0.5, 0.1875, ((1, 8),)),
    }


epsilon = 1e-06

def features(rows):
    width = rows.shape[-1]
    first, second = np.triu_indices(width)
    factor = jnp.asarray(np.where(first == second, 1.0, np.sqrt(2.0)), jnp.float32)
    wide = rows.astype(jnp.float32)
    return (wide[:, first] * wide[:, second] * factor).astype(jnp.bfloat16)

def rms_scale(values, gain):
    mean_square = lax.optimization_barrier(jnp.mean(values * values, axis=-1, keepdims=True))
    return values * lax.rsqrt(mean_square + epsilon) * gain

def head_block(query, key, value, prior, gain):
    count = query.shape[0]
    scores = jnp.dot(query, key.T, preferred_element_type=jnp.float32)
    places = jnp.arange(count, dtype=jnp.int32)
    causal = places[:, None] >= places[None, :]
    weights = jnp.where(causal, scores * scores, 0.0).astype(jnp.bfloat16)
    inner = jnp.dot(weights, value, preferred_element_type=jnp.float32)
    outer = jnp.dot(features(query).astype(jnp.float32), prior, precision=lax.Precision.HIGHEST)
    state = jnp.dot(features(key).T, value, preferred_element_type=jnp.float32)
    mixed = rms_scale(inner + outer, gain).astype(jnp.bfloat16)
    return (mixed, state)

def reference(residual, input_gain, project_in, output_gain, project_out):
    for layer in range(LAYERS):
        wide = residual.astype(jnp.float32)
        normed = rms_scale(wide, input_gain[layer]).astype(jnp.bfloat16)
        shaped = []
        for which in range(3):
            field = jnp.dot(normed, project_in[layer, which], preferred_element_type=jnp.float32).astype(jnp.bfloat16)
            shaped.append(field.reshape(N_CTX, CTX_TOK, HEADS, HD).transpose(0, 2, 1, 3))
        gains = output_gain[layer].reshape(HEADS, HD)

        def shard_step(prior, inputs):
            query, key, value = inputs
            mixed, state = jax.vmap(head_block)(query, key, value, prior, gains)
            return (prior + state, mixed)
        initial = jnp.zeros((HEADS, FEAT, HD), jnp.float32)
        ending, mixed = lax.scan(shard_step, initial, (shaped[0], shaped[1], shaped[2]))
        merged = mixed.transpose(0, 2, 1, 3).reshape(TOKENS, HEADS * HD)
        delta = jnp.dot(merged, project_out[layer], preferred_element_type=jnp.float32)
        residual = (wide + delta).astype(jnp.bfloat16)
    return residual
```

```python
import functools

import jax
import jax.numpy as jnp
from jax import lax
from jax.experimental import pallas as pl
from jax.experimental.pallas import tpu as pltpu
from jax.sharding import PartitionSpec as P

MESH = pl.DeviceIdType.MESH
D = 1024
HD = 64
LAYERS = 2
TOK = 256
NZ = 8
NY = 4
NX = 4
NH = 8
ROWS = TOK // NH
PAIRS = 9
PART = PAIRS * 8
SLICE = NZ * PART
EPS = 1e-06
F32 = jnp.float32
BF16 = jnp.bfloat16
FAR = (1, 3, 2)


def mm(a, b):
    return jnp.dot(a, b, preferred_element_type=F32)


def kernel(
    residual,
    in_gain,
    w_in,
    out_gain,
    w_out,
    result,
    rows_buf,
    win_buf,
    wout_buf,
    kv_buf,
    k_buf,
    q_buf,
    wide_k,
    wide_q,
    feat_k,
    feat_q,
    state,
    state_out,
    state_in,
    prior_out,
    prior_in,
    part_out,
    part_in,
    mix_buf,
    mix_in,
    q_rows,
    inner,
    resid,
    local_sem,
    rows_send,
    rows_recv,
    wout_send,
    wout_recv,
    kv_send,
    kv_recv,
    k_send,
    k_recv,
    q_send,
    q_recv,
    state_send,
    state_recv,
    prior_send,
    prior_recv,
    part_send,
    part_recv,
    mix_send,
    mix_recv,
    last_send,
    last_recv,
):
    ctx = lax.axis_index("ctx")
    head = lax.axis_index("head")
    z, y = ctx // NY, ctx % NY
    x, core = head // 2, head % 2
    sibling = x * 2 + (1 - core)

    def at_x(step):
        return ((x + step) % NX) * 2 + core

    def at_y(step):
        return z * NY + (y + step) % NY

    def at_z(step):
        return ((z + step) % NZ) * NY + y

    def send(src, dst, ssem, rsem, to):
        copy = pltpu.make_async_remote_copy(
            src_ref=src, dst_ref=dst, send_sem=ssem, recv_sem=rsem, device_id=to, device_id_type=MESH
        )
        copy.start()
        return copy

    own_rows = pltpu.make_async_copy(residual, rows_buf.at[head], local_sem.at[0])
    own_rows.start()
    loads = []
    for layer in range(LAYERS):
        for m in range(3):
            load = pltpu.make_async_copy(
                w_in.at[layer, m], win_buf.at[layer, :, pl.ds(m * 128, 128)], local_sem.at[1 + layer * 3 + m]
            )
            load.start()
            loads.append(load)
    own_out = []
    for layer in range(LAYERS):
        load = pltpu.make_async_copy(w_out.at[layer], wout_buf.at[layer, head], local_sem.at[7 + layer])
        load.start()
        own_out.append(load)

    barrier = pltpu.get_barrier_semaphore()
    for step in range(1, NH):
        pl.semaphore_signal(barrier, inc=1, device_id=(ctx, (head + step) % NH), device_id_type=MESH)
    for step in range(1, NY):
        pl.semaphore_signal(barrier, inc=1, device_id=(at_y(step), head), device_id_type=MESH)
    for step in range(1, NZ):
        pl.semaphore_signal(barrier, inc=1, device_id=(at_z(step), head), device_id_type=MESH)
    pl.semaphore_wait(barrier, NH - 1 + NY - 1 + NZ - 1)

    def gather_start(buf, ssem, rsem):
        mine = buf.at[head]
        copies = [send(mine, mine, ssem.at[0], rsem.at[0], (ctx, sibling))]
        for step in FAR:
            copies.append(send(mine, mine, ssem.at[step], rsem.at[step], (ctx, at_x(step))))
        return copies

    def gather_forward(buf, ssem, rsem, copies):
        more = []
        for place, step in enumerate(FAR):
            copies[1 + place].wait_recv()
            got = buf.at[at_x(NX - step)]
            more.append(send(got, got, ssem.at[3 + step], rsem.at[3 + step], (ctx, sibling)))
        return more

    def gather_end(copies, more):
        copies[0].wait_recv()
        for copy in more:
            copy.wait_recv()
        for copy in copies + more:
            copy.wait_send()

    own_rows.wait()
    copies = gather_start(rows_buf, rows_send, rows_recv)
    more = gather_forward(rows_buf, rows_send, rows_recv, copies)
    gather_end(copies, more)
    resid[...] = rows_buf[...].reshape(TOK, D).astype(F32)

    lane = lax.broadcasted_iota(jnp.int32, (1, 128), 1)
    low = lane < HD

    def block_pair(p):
        if p < 8:
            first = 2 * y + p // 4
            return first, (first + p % 4) % 8, (1.0 if p % 4 == 0 else 2.0)
        return y, y + 4, 2.0

    def make_features(wide, feat, slot):
        def head_features(h, carry):
            base = h * HD
            for p in range(PAIRS):
                one, other, _ = block_pair(p)
                block = wide[slot, pl.ds(pl.multiple_of(base + other * 8, 8), 8), :]
                for rr in range(4):
                    pieces = []
                    for o in range(2):
                        row = wide[slot, pl.ds(base + one * 8 + rr * 2 + o, 1), :]
                        pieces.append(block * row)
                    feat[h, pl.ds((rr * PAIRS + p) * 16, 16), pl.ds(slot * TOK, TOK)] = jnp.concatenate(
                        pieces, axis=0
                    ).astype(BF16)
            return carry

        lax.fori_loop(0, 2, head_features, 0)

    for layer in range(LAYERS):
        if layer == 0:
            own_out[0].wait()
            wout_first = gather_start(wout_buf.at[0], wout_send.at[0], wout_recv.at[0])
        wide = resid[...]
        mean_square = jnp.mean(wide * wide, axis=1, keepdims=True)
        normed = (wide * lax.rsqrt(mean_square + EPS) * in_gain[pl.ds(layer, 1), :]).astype(BF16)
        for m in range(3):
            loads[layer * 3 + m].wait()
        fields = mm(normed, win_buf[layer])
        query = fields[:, :128].astype(BF16).astype(F32)
        key = fields[:, 128:256].astype(BF16).astype(F32)
        kv_buf[layer, 0] = fields[:, 256:].astype(BF16)
        key_t = key.T
        k_buf[layer, 0] = key_t.astype(BF16)
        exchange = {}
        for step in FAR:
            to = (at_y(step), head)
            exchange["k", step] = send(
                k_buf.at[layer, 0], k_buf.at[layer, step], k_send.at[layer, step], k_recv.at[layer, step], to
            )
            exchange["v", step] = send(
                kv_buf.at[layer, 0], kv_buf.at[layer, step], kv_send.at[layer, step], kv_recv.at[layer, step], to
            )
        query_t = query.T
        q_buf[layer, 0] = query_t.astype(BF16)
        for step in FAR:
            to = (at_y(step), head)
            exchange["q", step] = send(
                q_buf.at[layer, 0], q_buf.at[layer, step], q_send.at[layer, step], q_recv.at[layer, step], to
            )
        q_rows[pl.ds(0, TOK), :] = jnp.where(low, query, 0.0).astype(BF16)
        q_rows[pl.ds(TOK, TOK), :] = jnp.where(low, 0.0, query).astype(BF16)

        for step in (0,) + FAR:
            if step == 0:
                wide_k[0] = key_t
            else:
                exchange["k", step].wait_recv()
                exchange["v", step].wait_recv()
                wide_k[step] = k_buf[layer, step].astype(F32)
            make_features(wide_k, feat_k, step)
            for h in range(2):
                term = mm(feat_k[h, :, pl.ds(step * TOK, TOK)], kv_buf[layer, step])
                if step == 0:
                    state[h] = term
                else:
                    state[h] += term
        for r in range(NZ):
            pieces = []
            for p in range(PAIRS):
                at = ((r // 2) * PAIRS + p) * 16 + (r % 2) * 8
                both = jnp.where(low, state[0, pl.ds(at, 8), :], state[1, pl.ds(at, 8), :])
                factor = block_pair(p)[2]
                pieces.append(both * factor if factor != 1.0 else both)
            state_out[layer, r] = jnp.concatenate(pieces, axis=0).astype(BF16)
        for step in range(1, NZ):
            exchange["s", step] = send(
                state_out.at[layer, (z + step) % NZ],
                state_in.at[layer, z],
                state_send.at[layer, step],
                state_recv.at[layer, step],
                (at_z(step), head),
            )
        state_in[layer, z] = state_out[layer, z]

        def attend(step):
            scores = mm(q_rows[...], k_buf[layer, step])
            weights = scores * scores
            if step == 0:
                row = lax.broadcasted_iota(jnp.int32, weights.shape, 0) % TOK
                column = lax.broadcasted_iota(jnp.int32, weights.shape, 1)
                weights = jnp.where(row >= column, weights, 0.0)
            return mm(weights.astype(BF16), kv_buf[layer, step])

        inner[...] = attend(0)

        for step in (0,) + FAR:
            if step == 0:
                wide_q[0] = query_t
            else:
                exchange["q", step].wait_recv()
                wide_q[step] = q_buf[layer, step].astype(F32)
            make_features(wide_q, feat_q, step)

        for step in range(1, NZ):
            exchange["s", step].wait_recv()
        running = jnp.zeros((PART, 128), F32)
        for row in range(NZ):
            prior_out[layer, row] = running.astype(BF16)
            if row < NZ - 1:
                running = running + state_in[layer, row].astype(F32)
        for step in range(1, NZ):
            exchange["p", step] = send(
                prior_out.at[layer, (z + step) % NZ],
                prior_in.at[layer, z],
                prior_send.at[layer, step],
                prior_recv.at[layer, step],
                (at_z(step), head),
            )
        prior_in[layer, z] = prior_out[layer, z]

        for step in range(1, NY):

            @pl.when(y >= step)
            def _(step=step):
                inner[...] += attend(step)

        if layer == 0:
            wout_more = gather_forward(wout_buf.at[0], wout_send.at[0], wout_recv.at[0], wout_first)
        else:
            wout_more = gather_forward(wout_buf.at[1], wout_send.at[1], wout_recv.at[1], wout_second)
        inner_t = jnp.where(low, inner[pl.ds(0, TOK), :], inner[pl.ds(TOK, TOK), :]).T

        for step in range(1, NZ):
            exchange["p", step].wait_recv()
        parts = [prior_in[layer, r].astype(F32) for r in range(NZ)]
        pieces = []
        for rr in range(4):
            for p in range(PAIRS):
                for o in range(2):
                    pieces.append(parts[rr * 2 + o][p * 8 : p * 8 + 8])
        prior_t = jnp.concatenate(pieces, axis=0).T.astype(BF16)

        def apply(step):
            return jnp.concatenate(
                [mm(prior_t[h * HD : h * HD + HD], feat_q[h, :, pl.ds(step * TOK, TOK)]) for h in range(2)], axis=0
            )

        for step in FAR:
            part_out[layer, step] = apply(step).astype(BF16)
            exchange["o", step] = send(
                part_out.at[layer, step],
                part_in.at[layer, step],
                part_send.at[layer, step],
                part_recv.at[layer, step],
                (at_y(NY - step), head),
            )
        total = inner_t + apply(0)
        for step in FAR:
            exchange["o", step].wait_recv()
            total += part_in[layer, step].astype(F32)

        scaled = []
        for h in range(2):
            mine = total[h * HD : h * HD + HD]
            mean_square = jnp.mean(mine * mine, axis=0, keepdims=True)
            scaled.append(mine * lax.rsqrt(mean_square + EPS))
        mixed = (jnp.concatenate(scaled, axis=0).T * out_gain[pl.ds(layer, 1), :]).astype(BF16)

        if layer == 0:
            gather_end(wout_first, wout_more)
            mix_buf[head] = mixed
            copies = gather_start(mix_buf, mix_send, mix_recv)
            more = gather_forward(mix_buf, mix_send, mix_recv, copies)
            own_out[1].wait()
            wout_second = gather_start(wout_buf.at[1], wout_send.at[1], wout_recv.at[1])
            gather_end(copies, more)
            columns = jnp.concatenate([mix_buf[n] for n in range(NH)], axis=1)
            delta = mm(columns, wout_buf[0].reshape(D, D))
            resid[...] = (resid[...] + delta).astype(BF16).astype(F32)
        else:
            gather_end(wout_second, wout_more)
            mix_buf[0] = mixed
            copies = []
            for step in range(1, NH):
                to = (head + step) % NH
                copies.append(
                    send(
                        mix_buf.at[0, pl.ds(pl.multiple_of(to * ROWS, ROWS), ROWS)],
                        mix_in.at[head],
                        last_send.at[step],
                        last_recv.at[step],
                        (ctx, to),
                    )
                )
            mine = pl.ds(pl.multiple_of(head * ROWS, ROWS), ROWS)
            mix_in[head] = mix_buf[0, mine]
            for copy in copies:
                copy.wait_recv()
            columns = jnp.concatenate([mix_in[n] for n in range(NH)], axis=1)
            delta = mm(columns, wout_buf[1].reshape(D, D))
            result[...] = (resid[mine, :] + delta).astype(BF16)
            for copy in copies:
                copy.wait_send()
        for copy in exchange.values():
            copy.wait_send()


def per_device(residual, in_gain, w_in, out_gain, w_out):
    any_space = pl.BlockSpec(memory_space=pl.ANY)
    vmem = pl.BlockSpec(memory_space=pltpu.VMEM)
    dma = pltpu.SemaphoreType.DMA
    return pl.pallas_call(
        kernel,
        out_shape=jax.ShapeDtypeStruct((ROWS, D), BF16),
        in_specs=[any_space, vmem, any_space, vmem, any_space],
        out_specs=vmem,
        scratch_shapes=[
            pltpu.VMEM((NH, ROWS, D), BF16),
            pltpu.VMEM((LAYERS, D, 3 * 128), BF16),
            pltpu.VMEM((LAYERS, NH, 128, D), BF16),
            pltpu.VMEM((LAYERS, NY, TOK, 128), BF16),
            pltpu.VMEM((LAYERS, NY, 128, TOK), BF16),
            pltpu.VMEM((LAYERS, NY, 128, TOK), BF16),
            pltpu.VMEM((NY, 128, TOK), F32),
            pltpu.VMEM((NY, 128, TOK), F32),
            pltpu.VMEM((2, SLICE, NY * TOK), BF16),
            pltpu.VMEM((2, SLICE, NY * TOK), BF16),
            pltpu.VMEM((2, SLICE, 128), F32),
            pltpu.VMEM((LAYERS, NZ, PART, 128), BF16),
            pltpu.VMEM((LAYERS, NZ, PART, 128), BF16),
            pltpu.VMEM((LAYERS, NZ, PART, 128), BF16),
            pltpu.VMEM((LAYERS, NZ, PART, 128), BF16),
            pltpu.VMEM((LAYERS, NY, 128, TOK), BF16),
            pltpu.VMEM((LAYERS, NY, 128, TOK), BF16),
            pltpu.VMEM((NH, TOK, 128), BF16),
            pltpu.VMEM((NH, ROWS, 128), BF16),
            pltpu.VMEM((2 * TOK, 128), BF16),
            pltpu.VMEM((2 * TOK, 128), F32),
            pltpu.VMEM((TOK, D), F32),
            dma((9,)),
            dma((7,)),
            dma((7,)),
            dma((LAYERS, 7)),
            dma((LAYERS, 7)),
            dma((LAYERS, NY)),
            dma((LAYERS, NY)),
            dma((LAYERS, NY)),
            dma((LAYERS, NY)),
            dma((LAYERS, NY)),
            dma((LAYERS, NY)),
            dma((LAYERS, NZ)),
            dma((LAYERS, NZ)),
            dma((LAYERS, NZ)),
            dma((LAYERS, NZ)),
            dma((LAYERS, NY)),
            dma((LAYERS, NY)),
            dma((7,)),
            dma((7,)),
            dma((NH,)),
            dma((NH,)),
        ],
        compiler_params=pltpu.CompilerParams(
            collective_id=0, has_side_effects=True, vmem_limit_bytes=48 * 1024 * 1024
        ),
        cost_estimate=pl.CostEstimate(flops=1_500_000_000, bytes_accessed=3_000_000, transcendentals=0),
    )(residual, in_gain, w_in, out_gain, w_out)


def solution(mesh):
    return jax.shard_map(
        per_device,
        mesh=mesh,
        in_specs=(
            P(("ctx", "head"), None),
            P(),
            P(None, None, None, "head"),
            P(None, "head"),
            P(None, "head", None),
        ),
        out_specs=P(("ctx", "head"), None),
        check_vma=False,
    )
```

```python
import functools

import jax
import jax.numpy as jnp
from jax import lax
from jax.experimental import pallas as pl
from jax.experimental.pallas import tpu as pltpu
from jax.sharding import PartitionSpec as P

MESH = pl.DeviceIdType.MESH
D = 1024
HD = 64
LAYERS = 2
TOK = 256
NZ = 8
NY = 4
NX = 4
NH = 8
ROWS = TOK // NH
PAIRS = 9
PART = PAIRS * 8
SLICE = NZ * PART
EPS = 1e-06
F32 = jnp.float32
BF16 = jnp.bfloat16
FAR = (1, 3, 2)
ZFAR = (4, 3, 5, 2, 6, 1, 7)
HALF = TOK // 2
HROWS = ROWS // 2


def mm(a, b):
    return jnp.dot(a, b, preferred_element_type=F32)


def kernel(
    residual,
    in_gain_hbm,
    w_in,
    out_gain_hbm,
    w_out,
    result,
    in_gain,
    out_gain,
    rows_buf,
    win_buf,
    wout_buf,
    kv_buf,
    q_buf,
    wide_k,
    wide_q,
    feat_k,
    feat_q,
    state,
    state_out,
    state_in,
    prior_out,
    prior_in,
    part_out,
    part_in,
    mix_buf,
    last_out,
    last_in,
    q_rows,
    inner,
    resid,
    local_sem,
    rows_send,
    rows_recv,
    wout_send,
    wout_recv,
    kv_send,
    kv_recv,
    q_send,
    q_recv,
    state_send,
    state_recv,
    prior_send,
    prior_recv,
    part_send,
    part_recv,
    mix_send,
    mix_recv,
    last_send,
    last_recv,
):
    ctx = lax.axis_index("ctx")
    head = lax.axis_index("head")
    z, y = ctx // NY, ctx % NY
    x, core = head // 2, head % 2
    sibling = x * 2 + (1 - core)

    def at_x(step):
        return ((x + step) % NX) * 2 + core

    def at_y(step):
        return z * NY + (y + step) % NY

    def at_z(step):
        return ((z + step) % NZ) * NY + y

    def send(src, dst, ssem, rsem, to):
        copy = pltpu.make_async_remote_copy(
            src_ref=src, dst_ref=dst, send_sem=ssem, recv_sem=rsem, device_id=to, device_id_type=MESH
        )
        copy.start()
        return copy

    barrier = pltpu.get_barrier_semaphore()
    for step in ZFAR:
        pl.semaphore_signal(barrier, inc=1, device_id=(at_z(step), head), device_id_type=MESH)
    for step in range(1, NY):
        pl.semaphore_signal(barrier, inc=1, device_id=(at_y(step), head), device_id_type=MESH)
    for step in range(1, NH):
        pl.semaphore_signal(barrier, inc=1, device_id=(ctx, (head + step) % NH), device_id_type=MESH)

    def load(src, dst, place):
        copy = pltpu.make_async_copy(src, dst, local_sem.at[place])
        copy.start()
        return copy

    own_rows = [load(residual.at[pl.ds(f * HROWS, HROWS)], rows_buf.at[f, head], f) for f in range(2)]
    gains = [load(in_gain_hbm, in_gain, 2), load(out_gain_hbm, out_gain, 3)]
    loads = [
        [
            load(w_in.at[layer, m], win_buf.at[layer, :, pl.ds(m * 128, 128)], 4 + layer * 3 + m)
            for m in range(3)
        ]
        for layer in range(LAYERS)
    ]
    own_out = [load(w_out.at[layer], wout_buf.at[layer, head], 10 + layer) for layer in range(LAYERS)]

    pl.semaphore_wait(barrier, NH - 1 + NY - 1 + NZ - 1)

    def gather_start(buf, ssem, rsem):
        mine = buf.at[head]
        copies = [send(mine, mine, ssem.at[0], rsem.at[0], (ctx, sibling))]
        for step in FAR:
            copies.append(send(mine, mine, ssem.at[step], rsem.at[step], (ctx, at_x(step))))
        return copies

    def gather_forward(buf, ssem, rsem, copies):
        more = []
        for place, step in enumerate(FAR):
            copies[1 + place].wait_recv()
            got = buf.at[at_x(NX - step)]
            more.append(send(got, got, ssem.at[3 + step], rsem.at[3 + step], (ctx, sibling)))
        return more

    def gather_arrive(copies, more):
        copies[0].wait_recv()
        for copy in more:
            copy.wait_recv()

    lane = lax.broadcasted_iota(jnp.int32, (1, 128), 1)
    low = lane < HD

    def block_pair(p):
        if p < 8:
            first = 2 * y + p // 4
            return first, (first + p % 4) % 8, (1.0 if p % 4 == 0 else 2.0)
        return y, y + 4, 2.0

    def make_features(wide, feat, slot, which):
        def head_features(h, carry):
            base = h * HD
            for f in which:
                for p in range(PAIRS):
                    one, other, _ = block_pair(p)
                    block = wide[slot, f, pl.ds(pl.multiple_of(base + other * 8, 8), 8), :]
                    for rr in range(4):
                        pieces = []
                        for o in range(2):
                            row = wide[slot, f, pl.ds(base + one * 8 + rr * 2 + o, 1), :]
                            pieces.append(block * row)
                        feat[h, pl.ds((rr * PAIRS + p) * 16, 16), pl.ds(slot * TOK + f * HALF, HALF)] = (
                            jnp.concatenate(pieces, axis=0).astype(BF16)
                        )
            return carry

        lax.fori_loop(0, 2, head_features, 0)

    sent = []

    halves = []
    for f in range(2):
        own_rows[f].wait()
        halves.append(gather_start(rows_buf.at[f], rows_send.at[f], rows_recv.at[f]))
    more = [gather_forward(rows_buf.at[f], rows_send.at[f], rows_recv.at[f], halves[f]) for f in range(2)]
    for copy in gains:
        copy.wait()

    for layer in range(LAYERS):
        exchange = {}
        queries = []
        for f in range(2):
            part = pl.ds(f * HALF, HALF)
            gather_arrive(halves[f], more[f])
            sent.extend(halves[f] + more[f])
            if layer == 0:
                wide = rows_buf[f].reshape(HALF, D).astype(F32)
            else:
                columns = jnp.concatenate([mix_buf[f, n] for n in range(NH)], axis=1)
                delta = mm(columns, wout_buf[0].reshape(D, D))
                wide = (resid[part, :] + delta).astype(BF16).astype(F32)
            resid[part, :] = wide
            mean_square = jnp.mean(wide * wide, axis=1, keepdims=True)
            normed = (wide * lax.rsqrt(mean_square + EPS) * in_gain[pl.ds(layer, 1), :]).astype(BF16)
            if f == 0:
                for copy in loads[layer]:
                    copy.wait()
            fields = mm(normed, win_buf[layer])
            key_t = fields[:, 128:256].astype(BF16).astype(F32).T
            kv_buf[layer, 0, 0, f] = key_t.astype(BF16)
            kv_buf[layer, 0, 1, f] = fields[:, 256:].astype(BF16)
            for step in FAR:
                exchange["kv", step, f] = send(
                    kv_buf.at[layer, 0, :, f],
                    kv_buf.at[layer, step, :, f],
                    kv_send.at[layer, step, f],
                    kv_recv.at[layer, step, f],
                    (at_y(step), head),
                )
            query = fields[:, :128].astype(BF16).astype(F32)
            query_t = query.T
            q_buf[layer, 0, f] = query_t.astype(BF16)
            wide_q[0, f] = query_t
            wide_k[0, f] = key_t
            q_rows[part, :] = jnp.where(low, query, 0.0).astype(BF16)
            q_rows[pl.ds(TOK + f * HALF, HALF), :] = jnp.where(low, 0.0, query).astype(BF16)
        for step in FAR:
            exchange["q", step] = send(
                q_buf.at[layer, 0], q_buf.at[layer, step], q_send.at[layer, step], q_recv.at[layer, step], (at_y(step), head)
            )

        own_out[layer].wait()
        wout_copies = gather_start(wout_buf.at[layer], wout_send.at[layer], wout_recv.at[layer])

        def values(step):
            return kv_buf[layer, step, 1].reshape(TOK, 128)

        def add_state(step):
            for h in range(2):
                term = mm(feat_k[h, :, pl.ds(step * TOK, TOK)], values(step))
                if step == 0:
                    state[h] = term
                else:
                    state[h] += term

        make_features(wide_k, feat_k, 0, (0, 1))
        add_state(0)
        for f in range(2):
            for step in FAR:
                exchange["kv", step, f].wait_recv()
                wide_k[step, f] = kv_buf[layer, step, 0, f].astype(F32)
                make_features(wide_k, feat_k, step, (f,))
                if f == 1:
                    add_state(step)
        for r in range(NZ):
            pieces = []
            for p in range(PAIRS):
                at = ((r // 2) * PAIRS + p) * 16 + (r % 2) * 8
                both = jnp.where(low, state[0, pl.ds(at, 8), :], state[1, pl.ds(at, 8), :])
                factor = block_pair(p)[2]
                pieces.append(both * factor if factor != 1.0 else both)
            state_out[layer, r] = jnp.concatenate(pieces, axis=0).astype(BF16)
        for step in ZFAR:
            exchange["s", step] = send(
                state_out.at[layer, (z + step) % NZ],
                state_in.at[layer, z],
                state_send.at[layer, step],
                state_recv.at[layer, step],
                (at_z(step), head),
            )
        state_in[layer, z] = state_out[layer, z]

        def attend(step):
            keys = jnp.concatenate([kv_buf[layer, step, 0, 0], kv_buf[layer, step, 0, 1]], axis=1)
            scores = mm(q_rows[...], keys)
            weights = scores * scores
            if step == 0:
                row = lax.broadcasted_iota(jnp.int32, weights.shape, 0) % TOK
                column = lax.broadcasted_iota(jnp.int32, weights.shape, 1)

                def place(i):
                    return ((i % HALF) // HROWS) * ROWS + (i // HALF) * HROWS + i % HROWS

                weights = jnp.where(place(row) >= place(column), weights, 0.0)
            return mm(weights.astype(BF16), values(step))

        inner[...] = attend(0)

        for step in (0,) + FAR:
            if step != 0:
                exchange["q", step].wait_recv()
                for f in range(2):
                    wide_q[step, f] = q_buf[layer, step, f].astype(F32)
            make_features(wide_q, feat_q, step, (0, 1))

        for step in ZFAR:
            exchange["s", step].wait_recv()
        running = jnp.zeros((PART, 128), F32)
        for row in range(NZ):
            prior_out[layer, row] = running.astype(BF16)
            if row < NZ - 1:
                running = running + state_in[layer, row].astype(F32)
        for step in ZFAR:
            exchange["p", step] = send(
                prior_out.at[layer, (z + step) % NZ],
                prior_in.at[layer, z],
                prior_send.at[layer, step],
                prior_recv.at[layer, step],
                (at_z(step), head),
            )
        prior_in[layer, z] = prior_out[layer, z]

        for step in range(1, NY):

            @pl.when(y >= step)
            def _(step=step):
                inner[...] += attend(step)

        inner_t = jnp.where(low, inner[pl.ds(0, TOK), :], inner[pl.ds(TOK, TOK), :]).T

        for step in ZFAR:
            exchange["p", step].wait_recv()
        parts = [prior_in[layer, r].astype(F32) for r in range(NZ)]
        pieces = []
        for rr in range(4):
            for p in range(PAIRS):
                for o in range(2):
                    pieces.append(parts[rr * 2 + o][p * 8 : p * 8 + 8])
        prior_t = jnp.concatenate(pieces, axis=0).T.astype(BF16)

        def apply(step):
            return jnp.concatenate(
                [mm(prior_t[h * HD : h * HD + HD], feat_q[h, :, pl.ds(step * TOK, TOK)]) for h in range(2)], axis=0
            )

        def give(step, f):
            exchange["o", step, f] = send(
                part_out.at[layer, step, f],
                part_in.at[layer, step, f],
                part_send.at[layer, step, f],
                part_recv.at[layer, step, f],
                (at_y(NY - step), head),
            )

        for step in FAR:
            outer = apply(step).astype(BF16)
            part_out[layer, step, 0] = outer[:, :HALF]
            part_out[layer, step, 1] = outer[:, HALF:]
            give(step, 0)
        for step in FAR:
            give(step, 1)
        wout_more = gather_forward(wout_buf.at[layer], wout_send.at[layer], wout_recv.at[layer], wout_copies)
        sent.extend(wout_copies + wout_more)
        own = inner_t + apply(0)

        if layer == 0:
            gather_arrive(wout_copies, wout_more)
        halves, more = [], []
        for f in range(2):
            total = own[:, f * HALF : f * HALF + HALF]
            for step in FAR:
                exchange["o", step, f].wait_recv()
                total += part_in[layer, step, f].astype(F32)
            scaled = []
            for h in range(2):
                mine = total[h * HD : h * HD + HD]
                mean_square = jnp.mean(mine * mine, axis=0, keepdims=True)
                scaled.append(mine * lax.rsqrt(mean_square + EPS))
            mixed = (jnp.concatenate(scaled, axis=0).T * out_gain[pl.ds(layer, 1), :]).astype(BF16)
            if layer == 0:
                mix_buf[f, head] = mixed
                halves.append(gather_start(mix_buf.at[f], mix_send.at[f], mix_recv.at[f]))
            else:
                last_out[:, f] = mixed.reshape(NH, HROWS, 128)
        if layer == 0:
            more = [gather_forward(mix_buf.at[f], mix_send.at[f], mix_recv.at[f], halves[f]) for f in range(2)]
        else:
            copies = []
            for step in range(1, NH):
                to = (head + step) % NH
                copies.append(
                    send(last_out.at[to], last_in.at[head], last_send.at[step], last_recv.at[step], (ctx, to))
                )
            last_in[head] = last_out[head]
            gather_arrive(wout_copies, wout_more)
            mine = jnp.concatenate(
                [resid[pl.ds(pl.multiple_of(f * HALF + head * HROWS, HROWS), HROWS), :] for f in range(2)], axis=0
            )
            for copy in copies:
                copy.wait_recv()
            columns = jnp.concatenate([last_in[n].reshape(ROWS, 128) for n in range(NH)], axis=1)
            delta = mm(columns, wout_buf[1].reshape(D, D))
            result[...] = (mine + delta).astype(BF16)
            sent.extend(copies)
        sent.extend(exchange.values())
    for copy in sent:
        copy.wait_send()


def per_device(residual, in_gain, w_in, out_gain, w_out):
    hbm = pl.BlockSpec(memory_space=pltpu.HBM)
    vmem = pl.BlockSpec(memory_space=pltpu.VMEM)
    dma = pltpu.SemaphoreType.DMA
    return pl.pallas_call(
        kernel,
        out_shape=jax.ShapeDtypeStruct((ROWS, D), BF16),
        in_specs=[hbm] * 5,
        out_specs=vmem,
        scratch_shapes=[
            pltpu.VMEM((LAYERS, D), F32),
            pltpu.VMEM((LAYERS, 128), F32),
            pltpu.VMEM((2, NH, HROWS, D), BF16),
            pltpu.VMEM((LAYERS, D, 3 * 128), BF16),
            pltpu.VMEM((LAYERS, NH, 128, D), BF16),
            pltpu.VMEM((LAYERS, NY, 2, 2, 128, 128), BF16),
            pltpu.VMEM((LAYERS, NY, 2, 128, HALF), BF16),
            pltpu.VMEM((NY, 2, 128, HALF), F32),
            pltpu.VMEM((NY, 2, 128, HALF), F32),
            pltpu.VMEM((2, SLICE, NY * TOK), BF16),
            pltpu.VMEM((2, SLICE, NY * TOK), BF16),
            pltpu.VMEM((2, SLICE, 128), F32),
            pltpu.VMEM((LAYERS, NZ, PART, 128), BF16),
            pltpu.VMEM((LAYERS, NZ, PART, 128), BF16),
            pltpu.VMEM((LAYERS, NZ, PART, 128), BF16),
            pltpu.VMEM((LAYERS, NZ, PART, 128), BF16),
            pltpu.VMEM((LAYERS, NY, 2, 128, HALF), BF16),
            pltpu.VMEM((LAYERS, NY, 2, 128, HALF), BF16),
            pltpu.VMEM((2, NH, HALF, 128), BF16),
            pltpu.VMEM((NH, 2, HROWS, 128), BF16),
            pltpu.VMEM((NH, 2, HROWS, 128), BF16),
            pltpu.VMEM((2 * TOK, 128), BF16),
            pltpu.VMEM((2 * TOK, 128), F32),
            pltpu.VMEM((TOK, D), F32),
            dma((12,)),
            dma((2, 7)),
            dma((2, 7)),
            dma((LAYERS, 7)),
            dma((LAYERS, 7)),
            dma((LAYERS, NY, 2)),
            dma((LAYERS, NY, 2)),
            dma((LAYERS, NY)),
            dma((LAYERS, NY)),
            dma((LAYERS, NZ)),
            dma((LAYERS, NZ)),
            dma((LAYERS, NZ)),
            dma((LAYERS, NZ)),
            dma((LAYERS, NY, 2)),
            dma((LAYERS, NY, 2)),
            dma((2, 7)),
            dma((2, 7)),
            dma((NH,)),
            dma((NH,)),
        ],
        compiler_params=pltpu.CompilerParams(
            collective_id=0, has_side_effects=True, vmem_limit_bytes=40 * 1024 * 1024
        ),
        cost_estimate=pl.CostEstimate(flops=1_500_000_000, bytes_accessed=3_000_000, transcendentals=0),
    )(*[pltpu.with_memory_space_constraint(a, pltpu.HBM) for a in (residual, in_gain, w_in, out_gain, w_out)])


def solution(mesh):
    return jax.shard_map(
        per_device,
        mesh=mesh,
        in_specs=(
            P(("ctx", "head"), None),
            P(),
            P(None, None, None, "head"),
            P(None, "head"),
            P(None, "head", None),
        ),
        out_specs=P(("ctx", "head"), None),
        check_vma=False,
    )
```

```python
import functools

import jax
import jax.numpy as jnp
from jax import lax
from jax.experimental import pallas as pl
from jax.experimental.pallas import tpu as pltpu
from jax.sharding import PartitionSpec as P

MESH = pl.DeviceIdType.MESH
D = 1024
HD = 64
LAYERS = 2
TOK = 256
NZ = 8
NY = 4
NX = 4
NH = 8
ROWS = TOK // NH
PAIRS = 9
PART = PAIRS * 8
SLICE = NZ * PART
EPS = 1e-06
F32 = jnp.float32
BF16 = jnp.bfloat16
FAR = (1, 3, 2)
ZFAR = (4, 3, 5, 2, 6, 1, 7)
HALF = TOK // 2
HROWS = ROWS // 2


def mm(a, b):
    return jnp.dot(a, b, preferred_element_type=F32)


def kernel(
    residual,
    in_gain_hbm,
    w_in,
    out_gain_hbm,
    w_out,
    result,
    in_gain,
    out_gain,
    rows_buf,
    win_buf,
    wout_buf,
    kv_buf,
    q_buf,
    wide_k,
    wide_q,
    feat_k,
    feat_q,
    state,
    state_out,
    state_in,
    prior_out,
    prior_in,
    part_out,
    part_in,
    mix_buf,
    last_out,
    last_in,
    normed_buf,
    q_rows,
    inner,
    attended,
    resid,
    line_sem,
    local_sem,
    rows_send,
    rows_recv,
    wout_send,
    wout_recv,
    kv_send,
    kv_recv,
    q_send,
    q_recv,
    state_send,
    state_recv,
    prior_send,
    prior_recv,
    part_send,
    part_recv,
    mix_send,
    mix_recv,
    last_send,
    last_recv,
):
    ctx = lax.axis_index("ctx")
    head = lax.axis_index("head")
    z, y = ctx // NY, ctx % NY
    x, core = head // 2, head % 2
    sibling = x * 2 + (1 - core)

    def at_x(step):
        return ((x + step) % NX) * 2 + core

    def at_y(step):
        return z * NY + (y + step) % NY

    def at_z(step):
        return ((z + step) % NZ) * NY + y

    def remote(src, dst, ssem, rsem, to):
        return pltpu.make_async_remote_copy(
            src_ref=src, dst_ref=dst, send_sem=ssem, recv_sem=rsem, device_id=to, device_id_type=MESH
        )

    def send(src, dst, ssem, rsem, to):
        copy = remote(src, dst, ssem, rsem, to)
        copy.start()
        return copy

    barrier = pltpu.get_barrier_semaphore()


    def tell_line(from_above, from_below, reach):
        @pl.when(z >= reach)
        def _():
            pl.semaphore_signal(from_above, inc=1, device_id=(ctx - reach * NY, head), device_id_type=MESH)

        @pl.when(z < NZ - reach)
        def _():
            pl.semaphore_signal(from_below, inc=1, device_id=(ctx + reach * NY, head), device_id_type=MESH)

    def tell_round(n):
        tell_line(line_sem.at[n, 0], line_sem.at[n, 1], 2**n)

    def hear_round(n):
        @pl.when(z < NZ - 2**n)
        def _():
            pl.semaphore_wait(line_sem.at[n, 0], 1)

        @pl.when(z >= 2**n)
        def _():
            pl.semaphore_wait(line_sem.at[n, 1], 1)

    tell_line(barrier, barrier, 1)
    for step in range(1, NY):
        pl.semaphore_signal(barrier, inc=1, device_id=(at_y(step), head), device_id_type=MESH)
    for step in range(1, NH):
        pl.semaphore_signal(barrier, inc=1, device_id=(ctx, (head + step) % NH), device_id_type=MESH)

    def load(src, dst, place):
        copy = pltpu.make_async_copy(src, dst, local_sem.at[place])
        copy.start()
        return copy

    own_rows = [load(residual.at[pl.ds(f * HROWS, HROWS)], rows_buf.at[f, head], f) for f in range(2)]
    gains = [load(in_gain_hbm, in_gain, 2), load(out_gain_hbm, out_gain, 3)]
    loads = [
        [
            load(w_in.at[layer, m], win_buf.at[layer, :, pl.ds(m * 128, 128)], 4 + layer * 3 + m)
            for m in range(3)
        ]
        for layer in range(LAYERS)
    ]
    own_out = [load(w_out.at[layer], wout_buf.at[layer, head], 10 + layer) for layer in range(LAYERS)]

    pl.semaphore_wait(barrier, NH - 1 + NY - 1 + (z + NZ - 1) // NZ + (2 * NZ - 2 - z) // NZ)
    tell_round(0)

    def gather_start(buf, ssem, rsem):
        mine = buf.at[head]
        copies = [send(mine, mine, ssem.at[0], rsem.at[0], (ctx, sibling))]
        for step in FAR:
            copies.append(send(mine, mine, ssem.at[step], rsem.at[step], (ctx, at_x(step))))
        return copies

    def gather_forward(buf, ssem, rsem, copies):
        more = []
        for place, step in enumerate(FAR):
            copies[1 + place].wait_recv()
            got = buf.at[at_x(NX - step)]
            more.append(send(got, got, ssem.at[3 + step], rsem.at[3 + step], (ctx, sibling)))
        return more

    def gather_arrive(copies, more):
        copies[0].wait_recv()
        for copy in more:
            copy.wait_recv()

    lane = lax.broadcasted_iota(jnp.int32, (1, 128), 1)
    low = lane < HD

    def block_pair(p):
        if p < 8:
            first = 2 * y + p // 4
            return first, (first + p % 4) % 8, (1.0 if p % 4 == 0 else 2.0)
        return y, y + 4, 2.0

    def make_features(wide, feat, slot, which):
        def head_features(h, carry):
            base = h * HD
            for f in which:
                for p in range(PAIRS):
                    one, other, _ = block_pair(p)
                    block = wide[slot, f, pl.ds(pl.multiple_of(base + other * 8, 8), 8), :]
                    for rr in range(4):
                        pieces = []
                        for o in range(2):
                            row = wide[slot, f, pl.ds(base + one * 8 + rr * 2 + o, 1), :]
                            pieces.append(block * row)
                        feat[h, pl.ds((rr * PAIRS + p) * 16, 16), pl.ds(slot * TOK + f * HALF, HALF)] = (
                            jnp.concatenate(pieces, axis=0).astype(BF16)
                        )
            return carry

        lax.fori_loop(0, 2, head_features, 0)

    sent = []

    halves = []
    for f in range(2):
        own_rows[f].wait()
        halves.append(gather_start(rows_buf.at[f], rows_send.at[f], rows_recv.at[f]))
    more = [gather_forward(rows_buf.at[f], rows_send.at[f], rows_recv.at[f], halves[f]) for f in range(2)]
    for copy in gains:
        copy.wait()

    for layer in range(LAYERS):
        exchange = {}
        for f in range(2):
            part = pl.ds(f * HALF, HALF)
            gather_arrive(halves[f], more[f])
            sent.extend(halves[f] + more[f])
            if layer == 0:
                wide = rows_buf[f].reshape(HALF, D).astype(F32)
            else:
                columns = jnp.concatenate([mix_buf[f, n] for n in range(NH)], axis=1)
                delta = mm(columns, wout_buf[0].reshape(D, D))
                wide = (resid[part, :] + delta).astype(BF16).astype(F32)
            resid[part, :] = wide
            mean_square = jnp.mean(wide * wide, axis=1, keepdims=True)
            normed = (wide * lax.rsqrt(mean_square + EPS) * in_gain[pl.ds(layer, 1), :]).astype(BF16)
            if f == 0:
                for copy in loads[layer]:
                    copy.wait()
            normed_buf[part, :] = normed
            fields = mm(normed, win_buf[layer, :, 128:])
            key_t = fields[:, :128].astype(BF16).astype(F32).T
            kv_buf[layer, 0, 0, f] = key_t.astype(BF16)
            kv_buf[layer, 0, 1, f] = fields[:, 128:].astype(BF16)
            for step in FAR:
                exchange["kv", step, f] = send(
                    kv_buf.at[layer, 0, :, f],
                    kv_buf.at[layer, step, :, f],
                    kv_send.at[layer, step, f],
                    kv_recv.at[layer, step, f],
                    (at_y(step), head),
                )
            wide_k[0, f] = key_t
            if layer == 0 and f == 0:
                hear_round(0)
                tell_round(1)
        query = mm(normed_buf[...], win_buf[layer, :, :128]).astype(BF16).astype(F32)
        query_t = query.T
        for f in range(2):
            wide_q[0, f] = query_t[:, f * HALF : f * HALF + HALF]
            q_buf[layer, 0, f] = query_t[:, f * HALF : f * HALF + HALF].astype(BF16)
        q_rows[pl.ds(0, TOK), :] = jnp.where(low, query, 0.0).astype(BF16)
        q_rows[pl.ds(TOK, TOK), :] = jnp.where(low, 0.0, query).astype(BF16)
        for step in FAR:
            exchange["q", step] = send(
                q_buf.at[layer, 0], q_buf.at[layer, step], q_send.at[layer, step], q_recv.at[layer, step], (at_y(step), head)
            )

        own_out[layer].wait()
        wout_copies = gather_start(wout_buf.at[layer], wout_send.at[layer], wout_recv.at[layer])

        def values(step):
            return kv_buf[layer, step, 1].reshape(TOK, 128)

        def add_state(step):
            for h in range(2):
                term = mm(feat_k[h, :, pl.ds(step * TOK, TOK)], values(step))
                if step == 0:
                    state[h] = term
                else:
                    state[h] += term

        make_features(wide_k, feat_k, 0, (0, 1))
        add_state(0)
        if layer == 0:
            hear_round(1)
            tell_round(2)
        for f in range(2):
            for step in FAR:
                exchange["kv", step, f].wait_recv()
                wide_k[step, f] = kv_buf[layer, step, 0, f].astype(F32)
                make_features(wide_k, feat_k, step, (f,))
                if f == 1:
                    add_state(step)
        for r in range(NZ):
            pieces = []
            for p in range(PAIRS):
                at = ((r // 2) * PAIRS + p) * 16 + (r % 2) * 8
                both = jnp.where(low, state[0, pl.ds(at, 8), :], state[1, pl.ds(at, 8), :])
                factor = block_pair(p)[2]
                pieces.append(both * factor if factor != 1.0 else both)
            state_out[layer, r] = jnp.concatenate(pieces, axis=0).astype(BF16)
        if layer == 0:
            hear_round(2)
        for step in ZFAR:
            exchange["s", step] = send(
                state_out.at[layer, (z + step) % NZ],
                state_in.at[layer, z],
                state_send.at[layer, step],
                state_recv.at[layer, step],
                (at_z(step), head),
            )
        state_in[layer, z] = state_out[layer, z]

        def attend(step):
            keys = jnp.concatenate([kv_buf[layer, step, 0, 0], kv_buf[layer, step, 0, 1]], axis=1)
            scores = mm(q_rows[...], keys)
            weights = scores * scores
            if step == 0:
                row = lax.broadcasted_iota(jnp.int32, weights.shape, 0) % TOK
                column = lax.broadcasted_iota(jnp.int32, weights.shape, 1)

                def place(i):
                    return ((i % HALF) // HROWS) * ROWS + (i // HALF) * HROWS + i % HROWS

                weights = jnp.where(place(row) >= place(column), weights, 0.0)
            return mm(weights.astype(BF16), values(step))

        inner[...] = attend(0)

        for step in (0,) + FAR:
            if step != 0:
                exchange["q", step].wait_recv()
                for f in range(2):
                    wide_q[step, f] = q_buf[layer, step, f].astype(F32)
            make_features(wide_q, feat_q, step, (0, 1))

        for step in ZFAR:
            exchange["s", step].wait_recv()
        running = jnp.zeros((PART, 128), F32)
        for row in range(NZ):
            prior_out[layer, row] = running.astype(BF16)
            if row < NZ - 1:
                running = running + state_in[layer, row].astype(F32)

        def prior_copy(step):
            return remote(
                prior_out.at[layer, (z + step) % NZ],
                prior_in.at[layer, z],
                prior_send.at[layer, step],
                prior_recv.at[layer, step],
                (at_z(step), head),
            )

        for step in ZFAR:

            @pl.when((z + step) % NZ != 0)
            def _(step=step):
                prior_copy(step).start()

        prior_in[layer, z] = prior_out[layer, z]

        for step in range(1, NY):

            @pl.when(y >= step)
            def _(step=step):
                inner[...] += attend(step)

        attended[...] = jnp.where(low, inner[pl.ds(0, TOK), :], inner[pl.ds(TOK, TOK), :]).T

        def part_copy(step, f):
            return remote(
                part_out.at[layer, step, f],
                part_in.at[layer, step, f],
                part_send.at[layer, step, f],
                part_recv.at[layer, step, f],
                (at_y(NY - step), head),
            )

        @pl.when(z > 0)
        def _():
            for step in ZFAR:
                prior_copy(step).wait_recv()
            parts = [prior_in[layer, r].astype(F32) for r in range(NZ)]
            pieces = []
            for rr in range(4):
                for p in range(PAIRS):
                    for o in range(2):
                        pieces.append(parts[rr * 2 + o][p * 8 : p * 8 + 8])
            prior_t = jnp.concatenate(pieces, axis=0).T.astype(BF16)

            def apply(step):
                return jnp.concatenate(
                    [mm(prior_t[h * HD : h * HD + HD], feat_q[h, :, pl.ds(step * TOK, TOK)]) for h in range(2)], axis=0
                )

            for step in FAR:
                outer = apply(step).astype(BF16)
                part_out[layer, step, 0] = outer[:, :HALF]
                part_out[layer, step, 1] = outer[:, HALF:]
                part_copy(step, 0).start()
            for step in FAR:
                part_copy(step, 1).start()
            attended[...] += apply(0)

        wout_more = gather_forward(wout_buf.at[layer], wout_send.at[layer], wout_recv.at[layer], wout_copies)
        sent.extend(wout_copies + wout_more)
        if layer == 0:
            gather_arrive(wout_copies, wout_more)
        halves, more = [], []
        for f in range(2):
            part = pl.ds(f * HALF, HALF)

            @pl.when(z > 0)
            def _(f=f, part=part):
                for step in FAR:
                    part_copy(step, f).wait_recv()
                attended[:, part] += sum(part_in[layer, step, f].astype(F32) for step in FAR)

            total = attended[:, part]
            scaled = []
            for h in range(2):
                mine = total[h * HD : h * HD + HD]
                mean_square = jnp.mean(mine * mine, axis=0, keepdims=True)
                scaled.append(mine * lax.rsqrt(mean_square + EPS))
            mixed = (jnp.concatenate(scaled, axis=0).T * out_gain[pl.ds(layer, 1), :]).astype(BF16)
            if layer == 0:
                mix_buf[f, head] = mixed
                halves.append(gather_start(mix_buf.at[f], mix_send.at[f], mix_recv.at[f]))
            else:
                last_out[:, f] = mixed.reshape(NH, HROWS, 128)
        if layer == 0:
            more = [gather_forward(mix_buf.at[f], mix_send.at[f], mix_recv.at[f], halves[f]) for f in range(2)]
        else:
            copies = []
            for step in range(1, NH):
                to = (head + step) % NH
                copies.append(
                    send(last_out.at[to], last_in.at[head], last_send.at[step], last_recv.at[step], (ctx, to))
                )
            last_in[head] = last_out[head]
            gather_arrive(wout_copies, wout_more)
            mine = jnp.concatenate(
                [resid[pl.ds(pl.multiple_of(f * HALF + head * HROWS, HROWS), HROWS), :] for f in range(2)], axis=0
            )
            for copy in copies:
                copy.wait_recv()
            columns = jnp.concatenate([last_in[n].reshape(ROWS, 128) for n in range(NH)], axis=1)
            delta = mm(columns, wout_buf[1].reshape(D, D))
            result[...] = (mine + delta).astype(BF16)
            sent.extend(copies)
        sent.extend(exchange.values())
        for step in ZFAR:

            @pl.when((z + step) % NZ != 0)
            def _(step=step):
                prior_copy(step).wait_send()

        @pl.when(z > 0)
        def _():
            for f in range(2):
                for step in FAR:
                    part_copy(step, f).wait_send()

    for copy in sent:
        copy.wait_send()


def per_device(residual, in_gain, w_in, out_gain, w_out):
    hbm = pl.BlockSpec(memory_space=pltpu.HBM)
    vmem = pl.BlockSpec(memory_space=pltpu.VMEM)
    dma = pltpu.SemaphoreType.DMA
    return pl.pallas_call(
        kernel,
        out_shape=jax.ShapeDtypeStruct((ROWS, D), BF16),
        in_specs=[hbm] * 5,
        out_specs=vmem,
        scratch_shapes=[
            pltpu.VMEM((LAYERS, D), F32),
            pltpu.VMEM((LAYERS, 128), F32),
            pltpu.VMEM((2, NH, HROWS, D), BF16),
            pltpu.VMEM((LAYERS, D, 3 * 128), BF16),
            pltpu.VMEM((LAYERS, NH, 128, D), BF16),
            pltpu.VMEM((LAYERS, NY, 2, 2, 128, 128), BF16),
            pltpu.VMEM((LAYERS, NY, 2, 128, HALF), BF16),
            pltpu.VMEM((NY, 2, 128, HALF), F32),
            pltpu.VMEM((NY, 2, 128, HALF), F32),
            pltpu.VMEM((2, SLICE, NY * TOK), BF16),
            pltpu.VMEM((2, SLICE, NY * TOK), BF16),
            pltpu.VMEM((2, SLICE, 128), F32),
            pltpu.VMEM((LAYERS, NZ, PART, 128), BF16),
            pltpu.VMEM((LAYERS, NZ, PART, 128), BF16),
            pltpu.VMEM((LAYERS, NZ, PART, 128), BF16),
            pltpu.VMEM((LAYERS, NZ, PART, 128), BF16),
            pltpu.VMEM((LAYERS, NY, 2, 128, HALF), BF16),
            pltpu.VMEM((LAYERS, NY, 2, 128, HALF), BF16),
            pltpu.VMEM((2, NH, HALF, 128), BF16),
            pltpu.VMEM((NH, 2, HROWS, 128), BF16),
            pltpu.VMEM((NH, 2, HROWS, 128), BF16),
            pltpu.VMEM((TOK, D), BF16),
            pltpu.VMEM((2 * TOK, 128), BF16),
            pltpu.VMEM((2 * TOK, 128), F32),
            pltpu.VMEM((128, TOK), F32),
            pltpu.VMEM((TOK, D), F32),
            pltpu.SemaphoreType.REGULAR((3, 2)),
            dma((12,)),
            dma((2, 7)),
            dma((2, 7)),
            dma((LAYERS, 7)),
            dma((LAYERS, 7)),
            dma((LAYERS, NY, 2)),
            dma((LAYERS, NY, 2)),
            dma((LAYERS, NY)),
            dma((LAYERS, NY)),
            dma((LAYERS, NZ)),
            dma((LAYERS, NZ)),
            dma((LAYERS, NZ)),
            dma((LAYERS, NZ)),
            dma((LAYERS, NY, 2)),
            dma((LAYERS, NY, 2)),
            dma((2, 7)),
            dma((2, 7)),
            dma((NH,)),
            dma((NH,)),
        ],
        compiler_params=pltpu.CompilerParams(
            collective_id=0, has_side_effects=True, vmem_limit_bytes=40 * 1024 * 1024
        ),
        cost_estimate=pl.CostEstimate(flops=1_500_000_000, bytes_accessed=3_000_000, transcendentals=0),
    )(*[pltpu.with_memory_space_constraint(a, pltpu.HBM) for a in (residual, in_gain, w_in, out_gain, w_out)])


def solution(mesh):
    return jax.shard_map(
        per_device,
        mesh=mesh,
        in_specs=(
            P(("ctx", "head"), None),
            P(),
            P(None, None, None, "head"),
            P(None, "head"),
            P(None, "head", None),
        ),
        out_specs=P(("ctx", "head"), None),
        check_vma=False,
    )
```

```python
import functools

import jax
import jax.numpy as jnp
from jax import lax
from jax.experimental import pallas as pl
from jax.experimental.pallas import tpu as pltpu
from jax.sharding import PartitionSpec as P

MESH = pl.DeviceIdType.MESH
D = 1024
HD = 64
LAYERS = 2
TOK = 256
NZ = 8
NY = 4
NX = 4
NH = 8
ROWS = TOK // NH
PAIRS = 9
PART = PAIRS * 8
SLICE = NZ * PART
EPS = 1e-06
F32 = jnp.float32
BF16 = jnp.bfloat16
FAR = (1, 3, 2)
ZFAR = (4, 3, 5, 2, 6, 1, 7)
HALF = TOK // 2
HROWS = ROWS // 2


def mm(a, b):
    return jnp.dot(a, b, preferred_element_type=F32)


def mm_t(a, b):
    return lax.dot_general(a, b, (((1,), (1,)), ((), ())), preferred_element_type=F32)


def kernel(
    residual,
    in_gain_hbm,
    w_in,
    out_gain_hbm,
    w_out,
    result,
    in_gain,
    out_gain,
    rows_buf,
    win_buf,
    wout_buf,
    kv_out,
    kv_in,
    q_out,
    q_in,
    wide_k,
    wide_q,
    feat_k,
    feat_q,
    state,
    state_out,
    state_in,
    prior_out,
    prior_in,
    part_out,
    part_in,
    mix_buf,
    last_out,
    last_in,
    normed_buf,
    q_rows,
    inner,
    acc,
    resid,
    line_sem,
    local_sem,
    rows_send,
    rows_recv,
    wout_send,
    wout_recv,
    kv_send,
    kv_recv,
    q_send,
    q_recv,
    state_send,
    state_recv,
    prior_send,
    prior_recv,
    part_send,
    part_recv,
    mix_send,
    mix_recv,
    last_send,
    last_recv,
):
    ctx = lax.axis_index("ctx")
    head = lax.axis_index("head")
    z, y = ctx // NY, ctx % NY
    x, core = head // 2, head % 2
    mine, half = y % 2, y // 2
    sibling = x * 2 + (1 - core)

    def at_x(step):
        return ((x + step) % NX) * 2 + core

    def at_y(step):
        return z * NY + (y + step) % NY

    def at_z(step):
        return ((z + step) % NZ) * NY + y

    def remote(src, dst, ssem, rsem, to):
        return pltpu.make_async_remote_copy(
            src_ref=src, dst_ref=dst, send_sem=ssem, recv_sem=rsem, device_id=to, device_id_type=MESH
        )

    def send(src, dst, ssem, rsem, to):
        copy = remote(src, dst, ssem, rsem, to)
        copy.start()
        return copy

    barrier = pltpu.get_barrier_semaphore()


    def tell_line(from_above, from_below, reach):
        @pl.when(z >= reach)
        def _():
            pl.semaphore_signal(from_above, inc=1, device_id=(ctx - reach * NY, head), device_id_type=MESH)

        @pl.when(z < NZ - reach)
        def _():
            pl.semaphore_signal(from_below, inc=1, device_id=(ctx + reach * NY, head), device_id_type=MESH)

    def tell_round(n):
        tell_line(line_sem.at[n, 0], line_sem.at[n, 1], 2**n)

    def hear_round(n):
        @pl.when(z < NZ - 2**n)
        def _():
            pl.semaphore_wait(line_sem.at[n, 0], 1)

        @pl.when(z >= 2**n)
        def _():
            pl.semaphore_wait(line_sem.at[n, 1], 1)

    tell_line(barrier, barrier, 1)
    for step in range(1, NY):
        pl.semaphore_signal(barrier, inc=1, device_id=(at_y(step), head), device_id_type=MESH)
    for step in range(1, NH):
        pl.semaphore_signal(barrier, inc=1, device_id=(ctx, (head + step) % NH), device_id_type=MESH)

    def load(src, dst, place):
        copy = pltpu.make_async_copy(src, dst, local_sem.at[place])
        copy.start()
        return copy

    own_rows = [load(residual.at[pl.ds(f * HROWS, HROWS)], rows_buf.at[f, head], f) for f in range(2)]
    gains = [load(in_gain_hbm, in_gain, 2), load(out_gain_hbm, out_gain, 3)]
    loads = [
        [
            load(w_in.at[layer, m], win_buf.at[layer, :, pl.ds(m * 128, 128)], 4 + layer * 3 + m)
            for m in range(3)
        ]
        for layer in range(LAYERS)
    ]
    own_out = [load(w_out.at[layer], wout_buf.at[layer, head], 10 + layer) for layer in range(LAYERS)]

    pl.semaphore_wait(barrier, NH - 1 + NY - 1 + (z + NZ - 1) // NZ + (2 * NZ - 2 - z) // NZ)
    tell_round(0)

    def gather_start(buf, ssem, rsem):
        mine = buf.at[head]
        copies = [send(mine, mine, ssem.at[0], rsem.at[0], (ctx, sibling))]
        for step in FAR:
            copies.append(send(mine, mine, ssem.at[step], rsem.at[step], (ctx, at_x(step))))
        return copies

    def gather_forward(buf, ssem, rsem, copies):
        more = []
        for place, step in enumerate(FAR):
            copies[1 + place].wait_recv()
            got = buf.at[at_x(NX - step)]
            more.append(send(got, got, ssem.at[3 + step], rsem.at[3 + step], (ctx, sibling)))
        return more

    def gather_arrive(copies, more):
        copies[0].wait_recv()
        for copy in more:
            copy.wait_recv()

    lane = lax.broadcasted_iota(jnp.int32, (1, 128), 1)
    low = lane < HD

    def factor(p):
        return 1.0 if p < 8 and p % 4 == 0 else 2.0

    def make_features(wide, feat, slot, which):
        def quarter_features(g, carry):
            quarter = 2 * half + g
            for f in which:
                for p in range(PAIRS):
                    if p < 8:
                        one = 2 * quarter + p // 4
                        other = (one + p % 4) % 8
                    else:
                        one, other = quarter, quarter + 4
                    block = wide[slot, f, pl.ds(pl.multiple_of(other * 8, 8), 8), :]
                    for rr in range(4):
                        pieces = []
                        for o in range(2):
                            row = wide[slot, f, pl.ds(one * 8 + rr * 2 + o, 1), :]
                            pieces.append(block * row)
                        feat[g, pl.ds((rr * PAIRS + p) * 16, 16), pl.ds(slot * TOK + f * HALF, HALF)] = (
                            jnp.concatenate(pieces, axis=0).astype(BF16)
                        )
            return carry

        lax.fori_loop(0, 2, quarter_features, 0)

    sent = []

    halves = []
    for f in range(2):
        own_rows[f].wait()
        halves.append(gather_start(rows_buf.at[f], rows_send.at[f], rows_recv.at[f]))
    more = [gather_forward(rows_buf.at[f], rows_send.at[f], rows_recv.at[f], halves[f]) for f in range(2)]
    for copy in gains:
        copy.wait()

    for layer in range(LAYERS):
        exchange = {}
        for f in range(2):
            part = pl.ds(f * HALF, HALF)
            gather_arrive(halves[f], more[f])
            sent.extend(halves[f] + more[f])
            if layer == 0:
                wide = rows_buf[f].reshape(HALF, D).astype(F32)
            else:
                columns = jnp.concatenate([mix_buf[f, n] for n in range(NH)], axis=1)
                delta = mm(columns, wout_buf[0].reshape(D, D))
                wide = (resid[part, :] + delta).astype(BF16).astype(F32)
            resid[part, :] = wide
            mean_square = jnp.mean(wide * wide, axis=1, keepdims=True)
            normed = (wide * lax.rsqrt(mean_square + EPS) * in_gain[pl.ds(layer, 1), :]).astype(BF16)
            if f == 0:
                for copy in loads[layer]:
                    copy.wait()
            normed_buf[part, :] = normed
            fields = mm(normed, win_buf[layer, :, 128:])
            fields_t = fields.astype(BF16).astype(F32).T
            for h in range(2):
                kv_out[layer, h, f] = jnp.concatenate(
                    [fields_t[h * HD : h * HD + HD], fields_t[128 + h * HD : 128 + h * HD + HD]], axis=0
                ).astype(BF16)
            for step in FAR:
                exchange["kv", step, f] = send(
                    kv_out.at[layer, (y + step) % 2, f],
                    kv_in.at[layer, step, f],
                    kv_send.at[layer, step, f],
                    kv_recv.at[layer, step, f],
                    (at_y(step), head),
                )
            own_kv = kv_out[layer, mine, f]
            kv_in[layer, 0, f] = own_kv
            wide_k[0, f] = own_kv[:HD].astype(F32)
            if layer == 0 and f == 0:
                hear_round(0)
                tell_round(1)
        query = mm(normed_buf[...], win_buf[layer, :, :128]).astype(BF16).astype(F32)
        query_t = query.T
        for h in range(2):
            for f in range(2):
                q_out[layer, h, f] = query_t[h * HD : h * HD + HD, f * HALF : f * HALF + HALF].astype(BF16)
        for step in FAR:
            exchange["q", step] = send(
                q_out.at[layer, (y + step) % 2],
                q_in.at[layer, step],
                q_send.at[layer, step],
                q_recv.at[layer, step],
                (at_y(step), head),
            )
        q_in[layer, 0] = q_out[layer, mine]
        own_out[layer].wait()
        wout_copies = gather_start(wout_buf.at[layer], wout_send.at[layer], wout_recv.at[layer])

        def keys(step):
            return jnp.concatenate([kv_in[layer, step, f, :HD] for f in range(2)], axis=1)

        def values(step):
            return jnp.concatenate([kv_in[layer, step, f, HD:] for f in range(2)], axis=1)

        def add_state(step):
            value = values(step)
            twice = jnp.concatenate([value, value], axis=0)
            for g in range(2):
                term = mm_t(feat_k[g, :, pl.ds(step * TOK, TOK)], twice)
                if step == 0:
                    state[g] = term
                else:
                    state[g] += term

        make_features(wide_k, feat_k, 0, (0, 1))
        add_state(0)
        if layer == 0:
            hear_round(1)
            tell_round(2)
        for f in range(2):
            for step in FAR:
                exchange["kv", step, f].wait_recv()
                wide_k[step, f] = kv_in[layer, step, f, :HD].astype(F32)
                make_features(wide_k, feat_k, step, (f,))
                if f == 1:
                    add_state(step)
        for r in range(NZ):
            pieces = []
            for p in range(PAIRS):
                at = ((r // 2) * PAIRS + p) * 16 + (r % 2) * 8
                both = jnp.where(low, state[0, pl.ds(at, 8), :], state[1, pl.ds(at, 8), :])
                pieces.append(both * factor(p))
            state_out[layer, r] = jnp.concatenate(pieces, axis=0).astype(BF16)
        if layer == 0:
            hear_round(2)
        for step in ZFAR:
            exchange["s", step] = send(
                state_out.at[layer, (z + step) % NZ],
                state_in.at[layer, z],
                state_send.at[layer, step],
                state_recv.at[layer, step],
                (at_z(step), head),
            )
        state_in[layer, z] = state_out[layer, z]

        for step in (0,) + FAR:
            if step != 0:
                exchange["q", step].wait_recv()
            for f in range(2):
                wide_q[step, f] = q_in[layer, step, f].astype(F32)
            make_features(wide_q, feat_q, step, (0, 1))
            q_rows[pl.ds(step * HALF, HALF), :] = wide_q[step, half].T.astype(BF16)

        def token(shard, i):
            return shard * TOK + ((i % HALF) // HROWS) * ROWS + (i // HALF) * HROWS + i % HROWS

        row = lax.broadcasted_iota(jnp.int32, (2 * TOK, 1), 0)
        row_token = token((y + NY - row // HALF) % NY, half * HALF + row % HALF)
        column = lax.broadcasted_iota(jnp.int32, (1, TOK), 1)

        def attend(step):
            scores = mm(q_rows[...], keys(step))
            column_token = token((y + NY - step) % NY, column)
            weights = jnp.where(row_token >= column_token, scores * scores, 0.0)
            return mm_t(weights.astype(BF16), values(step))

        inner[...] = attend(0)

        for step in ZFAR:
            exchange["s", step].wait_recv()
        running = jnp.zeros((PART, 128), F32)
        for row in range(NZ):
            prior_out[layer, row] = running.astype(BF16)
            if row < NZ - 1:
                running = running + state_in[layer, row].astype(F32)

        def prior_copy(step):
            return remote(
                prior_out.at[layer, (z + step) % NZ],
                prior_in.at[layer, z],
                prior_send.at[layer, step],
                prior_recv.at[layer, step],
                (at_z(step), head),
            )

        for step in ZFAR:

            @pl.when((z + step) % NZ != 0)
            def _(step=step):
                prior_copy(step).start()

        prior_in[layer, z] = prior_out[layer, z]

        for step in range(1, NY):
            inner[...] += attend(step)
        for step in range(NY):
            acc[step, half] = inner[pl.ds(step * HALF, HALF), :].T
            acc[step, 1 - half] = jnp.zeros((HD, HALF), F32)

        def part_copy(step, f):
            return remote(
                part_out.at[layer, step, f],
                part_in.at[layer, step, f],
                part_send.at[layer, step, f],
                part_recv.at[layer, step, f],
                (at_y(NY - step), head),
            )

        @pl.when(z > 0)
        def _():
            for step in ZFAR:
                prior_copy(step).wait_recv()
            parts = [prior_in[layer, r].astype(F32) for r in range(NZ)]
            pieces = []
            for rr in range(4):
                for p in range(PAIRS):
                    for o in range(2):
                        pieces.append(parts[rr * 2 + o][p * 8 : p * 8 + 8])
            prior_t = jnp.concatenate(pieces, axis=0).T.astype(BF16)

            def apply(step):
                columns = pl.ds(step * TOK, TOK)
                return mm(prior_t[:HD], feat_q[0, :, columns]) + mm(prior_t[HD:], feat_q[1, :, columns])

            for step in FAR:
                outer = apply(step)
                for f in range(2):
                    part_out[layer, step, f] = (acc[step, f] + outer[:, f * HALF : f * HALF + HALF]).astype(BF16)
                part_copy(step, 0).start()
            for step in FAR:
                part_copy(step, 1).start()
            outer = apply(0)
            for f in range(2):
                acc[0, f] += outer[:, f * HALF : f * HALF + HALF]

        @pl.when(z == 0)
        def _():
            for f in range(2):
                for step in FAR:
                    part_out[layer, step, f] = acc[step, f].astype(BF16)
                    part_copy(step, f).start()

        wout_more = gather_forward(wout_buf.at[layer], wout_send.at[layer], wout_recv.at[layer], wout_copies)
        sent.extend(wout_copies + wout_more)
        if layer == 0:
            gather_arrive(wout_copies, wout_more)
        halves, more = [], []
        for f in range(2):
            for step in FAR:
                part_copy(step, f).wait_recv()
            scaled = []
            for total in (
                acc[0, f] + part_in[layer, 2, f].astype(F32),
                part_in[layer, 1, f].astype(F32) + part_in[layer, 3, f].astype(F32),
            ):
                mean_square = jnp.mean(total * total, axis=0, keepdims=True)
                scaled.append(total * lax.rsqrt(mean_square + EPS))
            scaled = [jnp.where(mine == 0, scaled[0], scaled[1]), jnp.where(mine == 0, scaled[1], scaled[0])]
            mixed = (jnp.concatenate(scaled, axis=0).T * out_gain[pl.ds(layer, 1), :]).astype(BF16)
            if layer == 0:
                mix_buf[f, head] = mixed
                halves.append(gather_start(mix_buf.at[f], mix_send.at[f], mix_recv.at[f]))
            else:
                last_out[:, f] = mixed.reshape(NH, HROWS, 128)
        if layer == 0:
            more = [gather_forward(mix_buf.at[f], mix_send.at[f], mix_recv.at[f], halves[f]) for f in range(2)]
        else:
            copies = []
            for step in range(1, NH):
                to = (head + step) % NH
                copies.append(
                    send(last_out.at[to], last_in.at[head], last_send.at[step], last_recv.at[step], (ctx, to))
                )
            last_in[head] = last_out[head]
            gather_arrive(wout_copies, wout_more)
            before = jnp.concatenate(
                [resid[pl.ds(pl.multiple_of(f * HALF + head * HROWS, HROWS), HROWS), :] for f in range(2)], axis=0
            )
            for copy in copies:
                copy.wait_recv()
            columns = jnp.concatenate([last_in[n].reshape(ROWS, 128) for n in range(NH)], axis=1)
            delta = mm(columns, wout_buf[1].reshape(D, D))
            result[...] = (before + delta).astype(BF16)
            sent.extend(copies)
        sent.extend(exchange.values())
        for step in ZFAR:

            @pl.when((z + step) % NZ != 0)
            def _(step=step):
                prior_copy(step).wait_send()

        for f in range(2):
            for step in FAR:
                part_copy(step, f).wait_send()

    for copy in sent:
        copy.wait_send()


def per_device(residual, in_gain, w_in, out_gain, w_out):
    hbm = pl.BlockSpec(memory_space=pltpu.HBM)
    vmem = pl.BlockSpec(memory_space=pltpu.VMEM)
    dma = pltpu.SemaphoreType.DMA
    return pl.pallas_call(
        kernel,
        out_shape=jax.ShapeDtypeStruct((ROWS, D), BF16),
        in_specs=[hbm] * 5,
        out_specs=vmem,
        scratch_shapes=[
            pltpu.VMEM((LAYERS, D), F32),
            pltpu.VMEM((LAYERS, 128), F32),
            pltpu.VMEM((2, NH, HROWS, D), BF16),
            pltpu.VMEM((LAYERS, D, 3 * 128), BF16),
            pltpu.VMEM((LAYERS, NH, 128, D), BF16),
            pltpu.VMEM((LAYERS, 2, 2, 128, HALF), BF16),
            pltpu.VMEM((LAYERS, NY, 2, 128, HALF), BF16),
            pltpu.VMEM((LAYERS, 2, 2, HD, HALF), BF16),
            pltpu.VMEM((LAYERS, NY, 2, HD, HALF), BF16),
            pltpu.VMEM((NY, 2, HD, HALF), F32),
            pltpu.VMEM((NY, 2, HD, HALF), F32),
            pltpu.VMEM((2, SLICE, NY * TOK), BF16),
            pltpu.VMEM((2, SLICE, NY * TOK), BF16),
            pltpu.VMEM((2, SLICE, 128), F32),
            pltpu.VMEM((LAYERS, NZ, PART, 128), BF16),
            pltpu.VMEM((LAYERS, NZ, PART, 128), BF16),
            pltpu.VMEM((LAYERS, NZ, PART, 128), BF16),
            pltpu.VMEM((LAYERS, NZ, PART, 128), BF16),
            pltpu.VMEM((LAYERS, NY, 2, HD, HALF), BF16),
            pltpu.VMEM((LAYERS, NY, 2, HD, HALF), BF16),
            pltpu.VMEM((2, NH, HALF, 128), BF16),
            pltpu.VMEM((NH, 2, HROWS, 128), BF16),
            pltpu.VMEM((NH, 2, HROWS, 128), BF16),
            pltpu.VMEM((TOK, D), BF16),
            pltpu.VMEM((2 * TOK, HD), BF16),
            pltpu.VMEM((2 * TOK, HD), F32),
            pltpu.VMEM((NY, 2, HD, HALF), F32),
            pltpu.VMEM((TOK, D), F32),
            pltpu.SemaphoreType.REGULAR((3, 2)),
            dma((12,)),
            dma((2, 7)),
            dma((2, 7)),
            dma((LAYERS, 7)),
            dma((LAYERS, 7)),
            dma((LAYERS, NY, 2)),
            dma((LAYERS, NY, 2)),
            dma((LAYERS, NY)),
            dma((LAYERS, NY)),
            dma((LAYERS, NZ)),
            dma((LAYERS, NZ)),
            dma((LAYERS, NZ)),
            dma((LAYERS, NZ)),
            dma((LAYERS, NY, 2)),
            dma((LAYERS, NY, 2)),
            dma((2, 7)),
            dma((2, 7)),
            dma((NH,)),
            dma((NH,)),
        ],
        compiler_params=pltpu.CompilerParams(
            collective_id=0, has_side_effects=True, vmem_limit_bytes=40 * 1024 * 1024
        ),
        cost_estimate=pl.CostEstimate(flops=1_500_000_000, bytes_accessed=3_000_000, transcendentals=0),
    )(*[pltpu.with_memory_space_constraint(a, pltpu.HBM) for a in (residual, in_gain, w_in, out_gain, w_out)])


def solution(mesh):
    return jax.shard_map(
        per_device,
        mesh=mesh,
        in_specs=(
            P(("ctx", "head"), None),
            P(),
            P(None, None, None, "head"),
            P(None, "head"),
            P(None, "head", None),
        ),
        out_specs=P(("ctx", "head"), None),
        check_vma=False,
    )
```

```python
import functools

import jax
import jax.numpy as jnp
from jax import lax
from jax.experimental import pallas as pl
from jax.experimental.pallas import tpu as pltpu
from jax.sharding import PartitionSpec as P

MESH = pl.DeviceIdType.MESH
D = 1024
HD = 64
LAYERS = 2
TOK = 256
NZ = 8
NY = 4
NX = 4
NH = 8
ROWS = TOK // NH
PAIRS = 9
PART = PAIRS * 8
SLICE = NZ * PART
EPS = 1e-06
F32 = jnp.float32
BF16 = jnp.bfloat16
FAR = (1, 3, 2)
NEAR = 2
ZFAR = (4, 3, 5, 2, 6, 1, 7)
HALF = TOK // 2
HROWS = ROWS // 2


def mm(a, b):
    return jnp.dot(a, b, preferred_element_type=F32)


def mm_t(a, b):
    return lax.dot_general(a, b, (((1,), (1,)), ((), ())), preferred_element_type=F32)


def kernel(
    residual,
    in_gain_hbm,
    w_in,
    out_gain_hbm,
    w_out,
    result,
    in_gain,
    out_gain,
    rows_buf,
    win_buf,
    wout_buf,
    kv_out,
    kv_in,
    q_out,
    q_in,
    wide_k,
    wide_q,
    feat_k,
    feat_q,
    state,
    state_out,
    state_in,
    prior_out,
    prior_in,
    early_in,
    part_out,
    part_in,
    mix_buf,
    last_out,
    last_in,
    normed_buf,
    q_rows,
    inner,
    acc,
    resid,
    line_sem,
    local_sem,
    rows_send,
    rows_recv,
    wout_send,
    wout_recv,
    kv_send,
    kv_recv,
    q_send,
    q_recv,
    state_send,
    state_recv,
    prior_send,
    prior_recv,
    early_send,
    early_recv,
    part_send,
    part_recv,
    mix_send,
    mix_recv,
    last_send,
    last_recv,
):
    ctx = lax.axis_index("ctx")
    head = lax.axis_index("head")
    z, y = ctx // NY, ctx % NY
    x, core = head // 2, head % 2
    mine, half = y % 2, y // 2
    sibling = x * 2 + (1 - core)

    def at_x(step):
        return ((x + step) % NX) * 2 + core

    def at_y(step):
        return z * NY + (y + step) % NY

    def at_z(step):
        return ((z + step) % NZ) * NY + y

    def remote(src, dst, ssem, rsem, to):
        return pltpu.make_async_remote_copy(
            src_ref=src, dst_ref=dst, send_sem=ssem, recv_sem=rsem, device_id=to, device_id_type=MESH
        )

    def send(src, dst, ssem, rsem, to):
        copy = remote(src, dst, ssem, rsem, to)
        copy.start()
        return copy

    barrier = pltpu.get_barrier_semaphore()


    def tell_line(from_above, from_below, reach):
        @pl.when(z >= reach)
        def _():
            pl.semaphore_signal(from_above, inc=1, device_id=(ctx - reach * NY, head), device_id_type=MESH)

        @pl.when(z < NZ - reach)
        def _():
            pl.semaphore_signal(from_below, inc=1, device_id=(ctx + reach * NY, head), device_id_type=MESH)

    def tell_round(n):
        tell_line(line_sem.at[n, 0], line_sem.at[n, 1], 2**n)

    def hear_round(n):
        @pl.when(z < NZ - 2**n)
        def _():
            pl.semaphore_wait(line_sem.at[n, 0], 1)

        @pl.when(z >= 2**n)
        def _():
            pl.semaphore_wait(line_sem.at[n, 1], 1)

    tell_line(barrier, barrier, 1)
    for step in range(1, NY):
        pl.semaphore_signal(barrier, inc=1, device_id=(at_y(step), head), device_id_type=MESH)
    for step in range(1, NH):
        pl.semaphore_signal(barrier, inc=1, device_id=(ctx, (head + step) % NH), device_id_type=MESH)

    def load(src, dst, place):
        copy = pltpu.make_async_copy(src, dst, local_sem.at[place])
        copy.start()
        return copy

    own_rows = [load(residual.at[pl.ds(f * HROWS, HROWS)], rows_buf.at[f, head], f) for f in range(2)]
    gains = [load(in_gain_hbm, in_gain, 2), load(out_gain_hbm, out_gain, 3)]
    loads = [
        [
            load(w_in.at[layer, m], win_buf.at[layer, :, pl.ds(m * 128, 128)], 4 + layer * 3 + m)
            for m in range(3)
        ]
        for layer in range(LAYERS)
    ]
    own_out = [load(w_out.at[layer], wout_buf.at[layer, head], 10 + layer) for layer in range(LAYERS)]

    pl.semaphore_wait(barrier, NH - 1 + NY - 1 + (z + NZ - 1) // NZ + (2 * NZ - 2 - z) // NZ)
    tell_round(0)

    def gather_start(buf, ssem, rsem):
        mine = buf.at[head]
        copies = [send(mine, mine, ssem.at[0], rsem.at[0], (ctx, sibling))]
        for step in FAR:
            copies.append(send(mine, mine, ssem.at[step], rsem.at[step], (ctx, at_x(step))))
        return copies

    def gather_forward(buf, ssem, rsem, copies):
        more = []
        for place, step in enumerate(FAR):
            copies[1 + place].wait_recv()
            got = buf.at[at_x(NX - step)]
            more.append(send(got, got, ssem.at[3 + step], rsem.at[3 + step], (ctx, sibling)))
        return more

    def gather_arrive(copies, more):
        copies[0].wait_recv()
        for copy in more:
            copy.wait_recv()

    lane = lax.broadcasted_iota(jnp.int32, (1, 128), 1)
    low = lane < HD

    def factor(p):
        return 1.0 if p < 8 and p % 4 == 0 else 2.0

    def make_features(wide, feat, slot, which):
        def quarter_features(g, carry):
            quarter = 2 * half + g
            for f in which:
                for p in range(PAIRS):
                    if p < 8:
                        one = 2 * quarter + p // 4
                        other = (one + p % 4) % 8
                    else:
                        one, other = quarter, quarter + 4
                    block = wide[slot, f, pl.ds(pl.multiple_of(other * 8, 8), 8), :]
                    for rr in range(4):
                        pieces = []
                        for o in range(2):
                            row = wide[slot, f, pl.ds(one * 8 + rr * 2 + o, 1), :]
                            pieces.append(block * row)
                        feat[g, pl.ds((rr * PAIRS + p) * 16, 16), pl.ds(slot * TOK + f * HALF, HALF)] = (
                            jnp.concatenate(pieces, axis=0).astype(BF16)
                        )
            return carry

        lax.fori_loop(0, 2, quarter_features, 0)

    sent = []

    halves = []
    for f in range(2):
        own_rows[f].wait()
        halves.append(gather_start(rows_buf.at[f], rows_send.at[f], rows_recv.at[f]))
    more = [gather_forward(rows_buf.at[f], rows_send.at[f], rows_recv.at[f], halves[f]) for f in range(2)]
    for copy in gains:
        copy.wait()

    for layer in range(LAYERS):
        exchange = {}
        for f in range(2):
            part = pl.ds(f * HALF, HALF)
            gather_arrive(halves[f], more[f])
            sent.extend(halves[f] + more[f])
            if layer == 0:
                wide = rows_buf[f].reshape(HALF, D).astype(F32)
            else:
                columns = jnp.concatenate([mix_buf[f, n] for n in range(NH)], axis=1)
                delta = mm(columns, wout_buf[0].reshape(D, D))
                wide = (resid[part, :] + delta).astype(BF16).astype(F32)
            resid[part, :] = wide
            mean_square = jnp.mean(wide * wide, axis=1, keepdims=True)
            normed = (wide * lax.rsqrt(mean_square + EPS) * in_gain[pl.ds(layer, 1), :]).astype(BF16)
            if f == 0:
                for copy in loads[layer]:
                    copy.wait()
            normed_buf[part, :] = normed
            fields = mm(normed, win_buf[layer, :, 128:])
            fields_t = fields.astype(BF16).astype(F32).T
            for h in range(2):
                kv_out[layer, h, f] = jnp.concatenate(
                    [fields_t[h * HD : h * HD + HD], fields_t[128 + h * HD : 128 + h * HD + HD]], axis=0
                ).astype(BF16)
            for step in FAR:
                exchange["kv", step, f] = send(
                    kv_out.at[layer, (y + step) % 2, f],
                    kv_in.at[layer, step, f],
                    kv_send.at[layer, step, f],
                    kv_recv.at[layer, step, f],
                    (at_y(step), head),
                )
            own_kv = kv_out[layer, mine, f]
            kv_in[layer, 0, f] = own_kv
            wide_k[0, f] = own_kv[:HD].astype(F32)
            if layer == 0 and f == 0:
                hear_round(0)
                tell_round(1)
        query = mm(normed_buf[...], win_buf[layer, :, :128]).astype(BF16).astype(F32)
        query_t = query.T
        for h in range(2):
            for f in range(2):
                q_out[layer, h, f] = query_t[h * HD : h * HD + HD, f * HALF : f * HALF + HALF].astype(BF16)
        for step in FAR:
            exchange["q", step] = send(
                q_out.at[layer, (y + step) % 2],
                q_in.at[layer, step],
                q_send.at[layer, step],
                q_recv.at[layer, step],
                (at_y(step), head),
            )
        q_in[layer, 0] = q_out[layer, mine]
        own_out[layer].wait()
        wout_copies = gather_start(wout_buf.at[layer], wout_send.at[layer], wout_recv.at[layer])

        def keys(step):
            return jnp.concatenate([kv_in[layer, step, f, :HD] for f in range(2)], axis=1)

        def values(step):
            return jnp.concatenate([kv_in[layer, step, f, HD:] for f in range(2)], axis=1)

        def add_state(step):
            value = values(step)
            twice = jnp.concatenate([value, value], axis=0)
            for g in range(2):
                term = mm_t(feat_k[g, :, pl.ds(step * TOK, TOK)], twice)
                if step == 0:
                    state[g] = term
                else:
                    state[g] += term

        make_features(wide_k, feat_k, 0, (0, 1))
        add_state(0)
        if layer == 0:
            hear_round(1)
            tell_round(2)
        for f in range(2):
            for step in FAR:
                exchange["kv", step, f].wait_recv()
                wide_k[step, f] = kv_in[layer, step, f, :HD].astype(F32)
                make_features(wide_k, feat_k, step, (f,))
                if f == 1:
                    add_state(step)
        if layer == 0:
            hear_round(2)
        for step in ZFAR + (0,):
            r = (z + step) % NZ
            first = (r // 2) * (PAIRS * 16) + (r % 2) * 8
            pieces = []
            for p in range(PAIRS):
                rows = pl.ds(pl.multiple_of(first + p * 16, 8), 8)
                pieces.append(jnp.where(low, state[0, rows, :], state[1, rows, :]) * factor(p))
            state_out[layer, r] = jnp.concatenate(pieces, axis=0).astype(BF16)
            if step:
                exchange["s", step] = send(
                    state_out.at[layer, r],
                    state_in.at[layer, z],
                    state_send.at[layer, step],
                    state_recv.at[layer, step],
                    (at_z(step), head),
                )
        state_in[layer, z] = state_out[layer, z]

        def early_copy(reach):
            return remote(
                state_out.at[layer],
                early_in.at[layer, reach - 1],
                early_send.at[layer, reach - 1],
                early_recv.at[layer, reach - 1],
                (ctx + reach * NY, head),
            )

        for reach in range(1, NEAR):

            @pl.when(z < NEAR - reach)
            def _(reach=reach):
                early_copy(reach).start()


        for step in (0,) + FAR:
            if step != 0:
                exchange["q", step].wait_recv()
            for f in range(2):
                wide_q[step, f] = q_in[layer, step, f].astype(F32)
            make_features(wide_q, feat_q, step, (0, 1))
            q_rows[pl.ds(step * HALF, HALF), :] = wide_q[step, half].T.astype(BF16)

        def token(shard, i):
            return shard * TOK + ((i % HALF) // HROWS) * ROWS + (i // HALF) * HROWS + i % HROWS

        row = lax.broadcasted_iota(jnp.int32, (2 * TOK, 1), 0)
        row_token = token((y + NY - row // HALF) % NY, half * HALF + row % HALF)
        column = lax.broadcasted_iota(jnp.int32, (1, TOK), 1)

        def attend(step):
            scores = mm(q_rows[...], keys(step))
            column_token = token((y + NY - step) % NY, column)
            weights = jnp.where(row_token >= column_token, scores * scores, 0.0)
            return mm_t(weights.astype(BF16), values(step))

        inner[...] = attend(0)

        for step in ZFAR:
            exchange["s", step].wait_recv()
        running = jnp.zeros((PART, 128), F32)
        for row in range(NZ):
            prior_out[layer, row] = running.astype(BF16)
            if row < NZ - 1:
                running = running + state_in[layer, row].astype(F32)

        def prior_copy(step):
            return remote(
                prior_out.at[layer, (z + step) % NZ],
                prior_in.at[layer, z],
                prior_send.at[layer, step],
                prior_recv.at[layer, step],
                (at_z(step), head),
            )

        for step in ZFAR:

            @pl.when((z + step) % NZ >= NEAR)
            def _(step=step):
                prior_copy(step).start()

        prior_in[layer, z] = prior_out[layer, z]

        for step in range(1, NY):
            inner[...] += attend(step)
        for step in range(NY):
            acc[step, half] = inner[pl.ds(step * HALF, HALF), :].T
            acc[step, 1 - half] = jnp.zeros((HD, HALF), F32)

        def part_copy(step, f):
            return remote(
                part_out.at[layer, step, f],
                part_in.at[layer, step, f],
                part_send.at[layer, step, f],
                part_recv.at[layer, step, f],
                (at_y(NY - step), head),
            )

        @pl.when(z > 0)
        def _():
            @pl.when(z >= NEAR)
            def _():
                for step in ZFAR:
                    prior_copy(step).wait_recv()

            @pl.when(z < NEAR)
            def _():
                early_copy(1).wait_recv()
                prior_in[layer] = early_in[layer, 0]

            for reach in range(2, NEAR):

                @pl.when((z < NEAR) & (z >= reach))
                def _(reach=reach):
                    early_copy(reach).wait_recv()
                    prior_in[layer] = (prior_in[layer].astype(F32) + early_in[layer, reach - 1].astype(F32)).astype(BF16)

            parts = [prior_in[layer, r].astype(F32) for r in range(NZ)]
            pieces = []
            for rr in range(4):
                for p in range(PAIRS):
                    for o in range(2):
                        pieces.append(parts[rr * 2 + o][p * 8 : p * 8 + 8])
            prior_t = jnp.concatenate(pieces, axis=0).T.astype(BF16)

            def apply(step):
                columns = pl.ds(step * TOK, TOK)
                return mm(prior_t[:HD], feat_q[0, :, columns]) + mm(prior_t[HD:], feat_q[1, :, columns])

            for step in FAR:
                outer = apply(step)
                for f in range(2):
                    part_out[layer, step, f] = (acc[step, f] + outer[:, f * HALF : f * HALF + HALF]).astype(BF16)
                part_copy(step, 0).start()
            for step in FAR:
                part_copy(step, 1).start()
            outer = apply(0)
            for f in range(2):
                acc[0, f] += outer[:, f * HALF : f * HALF + HALF]

        @pl.when(z == 0)
        def _():
            for f in range(2):
                for step in FAR:
                    part_out[layer, step, f] = acc[step, f].astype(BF16)
                    part_copy(step, f).start()

        wout_more = gather_forward(wout_buf.at[layer], wout_send.at[layer], wout_recv.at[layer], wout_copies)
        sent.extend(wout_copies + wout_more)
        if layer == 0:
            gather_arrive(wout_copies, wout_more)
        halves, more = [], []
        for f in range(2):
            for step in FAR:
                part_copy(step, f).wait_recv()
            scaled = []
            for total in (
                acc[0, f] + part_in[layer, 2, f].astype(F32),
                part_in[layer, 1, f].astype(F32) + part_in[layer, 3, f].astype(F32),
            ):
                mean_square = jnp.mean(total * total, axis=0, keepdims=True)
                scaled.append(total * lax.rsqrt(mean_square + EPS))
            scaled = [jnp.where(mine == 0, scaled[0], scaled[1]), jnp.where(mine == 0, scaled[1], scaled[0])]
            mixed = (jnp.concatenate(scaled, axis=0).T * out_gain[pl.ds(layer, 1), :]).astype(BF16)
            if layer == 0:
                mix_buf[f, head] = mixed
                halves.append(gather_start(mix_buf.at[f], mix_send.at[f], mix_recv.at[f]))
            else:
                last_out[:, f] = mixed.reshape(NH, HROWS, 128)
        if layer == 0:
            more = [gather_forward(mix_buf.at[f], mix_send.at[f], mix_recv.at[f], halves[f]) for f in range(2)]
        else:
            copies = []
            for step in range(1, NH):
                to = (head + step) % NH
                copies.append(
                    send(last_out.at[to], last_in.at[head], last_send.at[step], last_recv.at[step], (ctx, to))
                )
            last_in[head] = last_out[head]
            gather_arrive(wout_copies, wout_more)
            before = jnp.concatenate(
                [resid[pl.ds(pl.multiple_of(f * HALF + head * HROWS, HROWS), HROWS), :] for f in range(2)], axis=0
            )
            for copy in copies:
                copy.wait_recv()
            columns = jnp.concatenate([last_in[n].reshape(ROWS, 128) for n in range(NH)], axis=1)
            delta = mm(columns, wout_buf[1].reshape(D, D))
            result[...] = (before + delta).astype(BF16)
            sent.extend(copies)
        sent.extend(exchange.values())
        for step in ZFAR:

            @pl.when((z + step) % NZ >= NEAR)
            def _(step=step):
                prior_copy(step).wait_send()

        for reach in range(1, NEAR):

            @pl.when(z < NEAR - reach)
            def _(reach=reach):
                early_copy(reach).wait_send()

        for f in range(2):
            for step in FAR:
                part_copy(step, f).wait_send()

    for copy in sent:
        copy.wait_send()


def per_device(residual, in_gain, w_in, out_gain, w_out):
    hbm = pl.BlockSpec(memory_space=pltpu.HBM)
    vmem = pl.BlockSpec(memory_space=pltpu.VMEM)
    dma = pltpu.SemaphoreType.DMA
    return pl.pallas_call(
        kernel,
        out_shape=jax.ShapeDtypeStruct((ROWS, D), BF16),
        in_specs=[hbm] * 5,
        out_specs=vmem,
        scratch_shapes=[
            pltpu.VMEM((LAYERS, D), F32),
            pltpu.VMEM((LAYERS, 128), F32),
            pltpu.VMEM((2, NH, HROWS, D), BF16),
            pltpu.VMEM((LAYERS, D, 3 * 128), BF16),
            pltpu.VMEM((LAYERS, NH, 128, D), BF16),
            pltpu.VMEM((LAYERS, 2, 2, 128, HALF), BF16),
            pltpu.VMEM((LAYERS, NY, 2, 128, HALF), BF16),
            pltpu.VMEM((LAYERS, 2, 2, HD, HALF), BF16),
            pltpu.VMEM((LAYERS, NY, 2, HD, HALF), BF16),
            pltpu.VMEM((NY, 2, HD, HALF), F32),
            pltpu.VMEM((NY, 2, HD, HALF), F32),
            pltpu.VMEM((2, SLICE, NY * TOK), BF16),
            pltpu.VMEM((2, SLICE, NY * TOK), BF16),
            pltpu.VMEM((2, SLICE, 128), F32),
            pltpu.VMEM((LAYERS, NZ, PART, 128), BF16),
            pltpu.VMEM((LAYERS, NZ, PART, 128), BF16),
            pltpu.VMEM((LAYERS, NZ, PART, 128), BF16),
            pltpu.VMEM((LAYERS, NZ, PART, 128), BF16),
            pltpu.VMEM((LAYERS, NEAR - 1, NZ, PART, 128), BF16),
            pltpu.VMEM((LAYERS, NY, 2, HD, HALF), BF16),
            pltpu.VMEM((LAYERS, NY, 2, HD, HALF), BF16),
            pltpu.VMEM((2, NH, HALF, 128), BF16),
            pltpu.VMEM((NH, 2, HROWS, 128), BF16),
            pltpu.VMEM((NH, 2, HROWS, 128), BF16),
            pltpu.VMEM((TOK, D), BF16),
            pltpu.VMEM((2 * TOK, HD), BF16),
            pltpu.VMEM((2 * TOK, HD), F32),
            pltpu.VMEM((NY, 2, HD, HALF), F32),
            pltpu.VMEM((TOK, D), F32),
            pltpu.SemaphoreType.REGULAR((3, 2)),
            dma((12,)),
            dma((2, 7)),
            dma((2, 7)),
            dma((LAYERS, 7)),
            dma((LAYERS, 7)),
            dma((LAYERS, NY, 2)),
            dma((LAYERS, NY, 2)),
            dma((LAYERS, NY)),
            dma((LAYERS, NY)),
            dma((LAYERS, NZ)),
            dma((LAYERS, NZ)),
            dma((LAYERS, NZ)),
            dma((LAYERS, NZ)),
            dma((LAYERS, NEAR - 1)),
            dma((LAYERS, NEAR - 1)),
            dma((LAYERS, NY, 2)),
            dma((LAYERS, NY, 2)),
            dma((2, 7)),
            dma((2, 7)),
            dma((NH,)),
            dma((NH,)),
        ],
        compiler_params=pltpu.CompilerParams(
            collective_id=0, has_side_effects=True, vmem_limit_bytes=40 * 1024 * 1024
        ),
        cost_estimate=pl.CostEstimate(flops=1_500_000_000, bytes_accessed=3_000_000, transcendentals=0),
    )(*[pltpu.with_memory_space_constraint(a, pltpu.HBM) for a in (residual, in_gain, w_in, out_gain, w_out)])


def solution(mesh):
    return jax.shard_map(
        per_device,
        mesh=mesh,
        in_specs=(
            P(("ctx", "head"), None),
            P(),
            P(None, None, None, "head"),
            P(None, "head"),
            P(None, "head", None),
        ),
        out_specs=P(("ctx", "head"), None),
        check_vma=False,
    )
```

```python
import functools

import jax
import jax.numpy as jnp
from jax import lax
from jax.experimental import pallas as pl
from jax.experimental.pallas import tpu as pltpu
from jax.sharding import PartitionSpec as P

MESH = pl.DeviceIdType.MESH
D = 1024
HD = 64
LAYERS = 2
TOK = 256
NZ = 8
NY = 4
NX = 4
NH = 8
ROWS = TOK // NH
PAIRS = 9
PART = PAIRS * 8
SLICE = NZ * PART
EPS = 1e-06
F32 = jnp.float32
BF16 = jnp.bfloat16
FAR = (1, 3, 2)
NEAR = 2
ZFAR = (4, 3, 5, 2, 6, 1, 7)
HALF = TOK // 2
HROWS = ROWS // 2


def mm(a, b):
    return jnp.dot(a, b, preferred_element_type=F32)


def mm_t(a, b):
    return lax.dot_general(a, b, (((1,), (1,)), ((), ())), preferred_element_type=F32)


def kernel(
    residual,
    in_gain_hbm,
    w_in,
    out_gain_hbm,
    w_out,
    result,
    in_gain,
    out_gain,
    rows_buf,
    win_buf,
    wout_buf,
    kv_out,
    kv_in,
    q_out,
    q_in,
    wide_k,
    wide_q,
    feat_k,
    feat_q,
    state,
    state_out,
    state_in,
    prior_out,
    prior_in,
    early_in,
    part_out,
    part_in,
    mix_buf,
    last_out,
    last_in,
    normed_buf,
    q_rows,
    inner,
    acc,
    resid,
    line_sem,
    local_sem,
    rows_send,
    rows_recv,
    wout_send,
    wout_recv,
    kv_send,
    kv_recv,
    q_send,
    q_recv,
    state_send,
    state_recv,
    prior_send,
    prior_recv,
    early_send,
    early_recv,
    part_send,
    part_recv,
    mix_send,
    mix_recv,
    last_send,
    last_recv,
):
    ctx = lax.axis_index("ctx")
    head = lax.axis_index("head")
    z, y = ctx // NY, ctx % NY
    x, core = head // 2, head % 2
    mine, half = y % 2, y // 2
    sibling = x * 2 + (1 - core)

    def at_x(step):
        return ((x + step) % NX) * 2 + core

    def at_y(step):
        return z * NY + (y + step) % NY

    def at_z(step):
        return ((z + step) % NZ) * NY + y

    def remote(src, dst, ssem, rsem, to):
        return pltpu.make_async_remote_copy(
            src_ref=src, dst_ref=dst, send_sem=ssem, recv_sem=rsem, device_id=to, device_id_type=MESH
        )

    def send(src, dst, ssem, rsem, to):
        copy = remote(src, dst, ssem, rsem, to)
        copy.start()
        return copy

    barrier = pltpu.get_barrier_semaphore()


    def tell_line(from_above, from_below, reach):
        @pl.when(z >= reach)
        def _():
            pl.semaphore_signal(from_above, inc=1, device_id=(ctx - reach * NY, head), device_id_type=MESH)

        @pl.when(z < NZ - reach)
        def _():
            pl.semaphore_signal(from_below, inc=1, device_id=(ctx + reach * NY, head), device_id_type=MESH)

    def tell_round(n):
        tell_line(line_sem.at[n, 0], line_sem.at[n, 1], 2**n)

    def hear_round(n):
        @pl.when(z < NZ - 2**n)
        def _():
            pl.semaphore_wait(line_sem.at[n, 0], 1)

        @pl.when(z >= 2**n)
        def _():
            pl.semaphore_wait(line_sem.at[n, 1], 1)

    tell_line(barrier, barrier, 1)
    for step in range(1, NY):
        pl.semaphore_signal(barrier, inc=1, device_id=(at_y(step), head), device_id_type=MESH)
    for step in range(1, NH):
        pl.semaphore_signal(barrier, inc=1, device_id=(ctx, (head + step) % NH), device_id_type=MESH)

    def load(src, dst, place):
        copy = pltpu.make_async_copy(src, dst, local_sem.at[place])
        copy.start()
        return copy

    own_rows = [load(residual.at[pl.ds(f * HROWS, HROWS)], rows_buf.at[f, head], f) for f in range(2)]
    gains = [load(in_gain_hbm, in_gain, 2), load(out_gain_hbm, out_gain, 3)]
    loads = [
        [
            load(w_in.at[layer, m], win_buf.at[layer, :, pl.ds(m * 128, 128)], 4 + layer * 3 + m)
            for m in range(3)
        ]
        for layer in range(LAYERS)
    ]
    own_out = [load(w_out.at[layer], wout_buf.at[layer, head], 10 + layer) for layer in range(LAYERS)]

    pl.semaphore_wait(barrier, NH - 1 + NY - 1 + (z + NZ - 1) // NZ + (2 * NZ - 2 - z) // NZ)
    tell_round(0)

    def gather_start(buf, ssem, rsem):
        mine = buf.at[head]
        copies = [send(mine, mine, ssem.at[0], rsem.at[0], (ctx, sibling))]
        for step in FAR:
            copies.append(send(mine, mine, ssem.at[step], rsem.at[step], (ctx, at_x(step))))
        return copies

    def gather_forward(buf, ssem, rsem, copies):
        more = []
        for place, step in enumerate(FAR):
            copies[1 + place].wait_recv()
            got = buf.at[at_x(NX - step)]
            more.append(send(got, got, ssem.at[3 + step], rsem.at[3 + step], (ctx, sibling)))
        return more

    def gather_arrive(copies, more):
        copies[0].wait_recv()
        for copy in more:
            copy.wait_recv()

    lane = lax.broadcasted_iota(jnp.int32, (1, 128), 1)
    low = lane < HD

    def factor(p):
        return 1.0 if p < 8 and p % 4 == 0 else 2.0

    def make_features(wide, feat, slot, which):
        def quarter_features(g, carry):
            quarter = 2 * half + g
            for f in which:
                for p in range(PAIRS):
                    if p < 8:
                        one = 2 * quarter + p // 4
                        other = (one + p % 4) % 8
                    else:
                        one, other = quarter, quarter + 4
                    block = wide[slot, f, pl.ds(pl.multiple_of(other * 8, 8), 8), :]
                    for rr in range(4):
                        pieces = []
                        for o in range(2):
                            row = wide[slot, f, pl.ds(one * 8 + rr * 2 + o, 1), :]
                            pieces.append(block * row)
                        feat[g, pl.ds((rr * PAIRS + p) * 16, 16), pl.ds(slot * TOK + f * HALF, HALF)] = (
                            jnp.concatenate(pieces, axis=0).astype(BF16)
                        )
            return carry

        lax.fori_loop(0, 2, quarter_features, 0)

    sent = []

    halves = []
    for f in range(2):
        own_rows[f].wait()
        halves.append(gather_start(rows_buf.at[f], rows_send.at[f], rows_recv.at[f]))
    more = [gather_forward(rows_buf.at[f], rows_send.at[f], rows_recv.at[f], halves[f]) for f in range(2)]
    for copy in gains:
        copy.wait()

    for layer in range(LAYERS):
        exchange = {}
        for f in range(2):
            part = pl.ds(f * HALF, HALF)
            sent.extend(halves[f] + more[f])
            if layer == 0:
                gather_arrive(halves[f], more[f])
                wide = rows_buf[f].reshape(HALF, D).astype(F32)
            else:
                delta = jnp.zeros((HALF, D), F32)
                for step, arrival in zip((0,) + FAR, halves[f][:1] + more[f]):
                    arrival.wait_recv()
                    chip = (x + NX - step) % NX
                    columns = jnp.concatenate([mix_buf[f, 2 * chip + c] for c in range(2)], axis=1)
                    delta += mm(columns, wout_buf[0, pl.ds(2 * chip, 2)].reshape(2 * 128, D))
                wide = (resid[part, :] + delta).astype(BF16).astype(F32)
            resid[part, :] = wide
            mean_square = jnp.mean(wide * wide, axis=1, keepdims=True)
            normed = (wide * lax.rsqrt(mean_square + EPS) * in_gain[pl.ds(layer, 1), :]).astype(BF16)
            if f == 0:
                for copy in loads[layer]:
                    copy.wait()
            normed_buf[part, :] = normed
            fields = mm(normed, win_buf[layer, :, 128:])
            fields_t = fields.astype(BF16).astype(F32).T
            for h in range(2):
                kv_out[layer, h, f] = jnp.concatenate(
                    [fields_t[h * HD : h * HD + HD], fields_t[128 + h * HD : 128 + h * HD + HD]], axis=0
                ).astype(BF16)
            for step in FAR:
                exchange["kv", step, f] = send(
                    kv_out.at[layer, (y + step) % 2, f],
                    kv_in.at[layer, step, f],
                    kv_send.at[layer, step, f],
                    kv_recv.at[layer, step, f],
                    (at_y(step), head),
                )
            own_kv = kv_out[layer, mine, f]
            kv_in[layer, 0, f] = own_kv
            wide_k[0, f] = own_kv[:HD].astype(F32)
            if layer == 0 and f == 0:
                hear_round(0)
                tell_round(1)
        query = mm(normed_buf[...], win_buf[layer, :, :128]).astype(BF16).astype(F32)
        query_t = query.T
        for h in range(2):
            for f in range(2):
                q_out[layer, h, f] = query_t[h * HD : h * HD + HD, f * HALF : f * HALF + HALF].astype(BF16)
        for step in FAR:
            exchange["q", step] = send(
                q_out.at[layer, (y + step) % 2],
                q_in.at[layer, step],
                q_send.at[layer, step],
                q_recv.at[layer, step],
                (at_y(step), head),
            )
        q_in[layer, 0] = q_out[layer, mine]
        own_out[layer].wait()
        wout_copies = gather_start(wout_buf.at[layer], wout_send.at[layer], wout_recv.at[layer])

        def keys(step):
            return jnp.concatenate([kv_in[layer, step, f, :HD] for f in range(2)], axis=1)

        def values(step):
            return jnp.concatenate([kv_in[layer, step, f, HD:] for f in range(2)], axis=1)

        def add_state(step):
            value = values(step)
            twice = jnp.concatenate([value, value], axis=0)
            for g in range(2):
                term = mm_t(feat_k[g, :, pl.ds(step * TOK, TOK)], twice)
                if step == 0:
                    state[g] = term
                else:
                    state[g] += term

        make_features(wide_k, feat_k, 0, (0, 1))
        add_state(0)
        if layer == 0:
            hear_round(1)
            tell_round(2)
        for f in range(2):
            for step in FAR:
                exchange["kv", step, f].wait_recv()
                wide_k[step, f] = kv_in[layer, step, f, :HD].astype(F32)
                make_features(wide_k, feat_k, step, (f,))
                if f == 1:
                    add_state(step)
        for r in range(NZ):
            pieces = []
            for p in range(PAIRS):
                at = ((r // 2) * PAIRS + p) * 16 + (r % 2) * 8
                both = jnp.where(low, state[0, pl.ds(at, 8), :], state[1, pl.ds(at, 8), :])
                pieces.append(both * factor(p))
            state_out[layer, r] = jnp.concatenate(pieces, axis=0).astype(BF16)
        if layer == 0:
            hear_round(2)
        for step in ZFAR:
            exchange["s", step] = send(
                state_out.at[layer, (z + step) % NZ],
                state_in.at[layer, z],
                state_send.at[layer, step],
                state_recv.at[layer, step],
                (at_z(step), head),
            )
        state_in[layer, z] = state_out[layer, z]

        def early_copy(reach):
            return remote(
                state_out.at[layer],
                early_in.at[layer, reach - 1],
                early_send.at[layer, reach - 1],
                early_recv.at[layer, reach - 1],
                (ctx + reach * NY, head),
            )

        for reach in range(1, NEAR):

            @pl.when(z < NEAR - reach)
            def _(reach=reach):
                early_copy(reach).start()


        for step in (0,) + FAR:
            if step != 0:
                exchange["q", step].wait_recv()
            for f in range(2):
                wide_q[step, f] = q_in[layer, step, f].astype(F32)
            make_features(wide_q, feat_q, step, (0, 1))
            q_rows[pl.ds(step * HALF, HALF), :] = wide_q[step, half].T.astype(BF16)

        def token(shard, i):
            return shard * TOK + ((i % HALF) // HROWS) * ROWS + (i // HALF) * HROWS + i % HROWS

        row = lax.broadcasted_iota(jnp.int32, (2 * TOK, 1), 0)
        row_token = token((y + NY - row // HALF) % NY, half * HALF + row % HALF)
        column = lax.broadcasted_iota(jnp.int32, (1, TOK), 1)

        def attend(step):
            scores = mm(q_rows[...], keys(step))
            column_token = token((y + NY - step) % NY, column)
            weights = jnp.where(row_token >= column_token, scores * scores, 0.0)
            return mm_t(weights.astype(BF16), values(step))

        inner[...] = attend(0)

        for step in ZFAR:
            exchange["s", step].wait_recv()
        running = jnp.zeros((PART, 128), F32)
        for row in range(NZ):
            prior_out[layer, row] = running.astype(BF16)
            if row < NZ - 1:
                running = running + state_in[layer, row].astype(F32)

        def prior_copy(step):
            return remote(
                prior_out.at[layer, (z + step) % NZ],
                prior_in.at[layer, z],
                prior_send.at[layer, step],
                prior_recv.at[layer, step],
                (at_z(step), head),
            )

        for step in ZFAR:

            @pl.when((z + step) % NZ >= NEAR)
            def _(step=step):
                prior_copy(step).start()

        prior_in[layer, z] = prior_out[layer, z]

        for step in range(1, NY):
            inner[...] += attend(step)
        for step in range(NY):
            acc[step, half] = inner[pl.ds(step * HALF, HALF), :].T
            acc[step, 1 - half] = jnp.zeros((HD, HALF), F32)

        def part_copy(step, f):
            return remote(
                part_out.at[layer, step, f],
                part_in.at[layer, step, f],
                part_send.at[layer, step, f],
                part_recv.at[layer, step, f],
                (at_y(NY - step), head),
            )

        @pl.when(z > 0)
        def _():
            @pl.when(z >= NEAR)
            def _():
                for step in ZFAR:
                    prior_copy(step).wait_recv()

            @pl.when(z < NEAR)
            def _():
                early_copy(1).wait_recv()
                prior_in[layer] = early_in[layer, 0]

            for reach in range(2, NEAR):

                @pl.when((z < NEAR) & (z >= reach))
                def _(reach=reach):
                    early_copy(reach).wait_recv()
                    prior_in[layer] = (prior_in[layer].astype(F32) + early_in[layer, reach - 1].astype(F32)).astype(BF16)

            parts = [prior_in[layer, r].astype(F32) for r in range(NZ)]
            pieces = []
            for rr in range(4):
                for p in range(PAIRS):
                    for o in range(2):
                        pieces.append(parts[rr * 2 + o][p * 8 : p * 8 + 8])
            prior_t = jnp.concatenate(pieces, axis=0).T.astype(BF16)

            def apply(step):
                columns = pl.ds(step * TOK, TOK)
                return mm(prior_t[:HD], feat_q[0, :, columns]) + mm(prior_t[HD:], feat_q[1, :, columns])

            for step in FAR:
                outer = apply(step)
                for f in range(2):
                    part_out[layer, step, f] = (acc[step, f] + outer[:, f * HALF : f * HALF + HALF]).astype(BF16)
                part_copy(step, 0).start()
            for step in FAR:
                part_copy(step, 1).start()
            outer = apply(0)
            for f in range(2):
                acc[0, f] += outer[:, f * HALF : f * HALF + HALF]

        @pl.when(z == 0)
        def _():
            for f in range(2):
                for step in FAR:
                    part_out[layer, step, f] = acc[step, f].astype(BF16)
                    part_copy(step, f).start()

        wout_more = gather_forward(wout_buf.at[layer], wout_send.at[layer], wout_recv.at[layer], wout_copies)
        sent.extend(wout_copies + wout_more)
        if layer == 0:
            gather_arrive(wout_copies, wout_more)
        halves, more = [], []
        for f in range(2):
            for step in FAR:
                part_copy(step, f).wait_recv()
            scaled = []
            for total in (
                acc[0, f] + part_in[layer, 2, f].astype(F32),
                part_in[layer, 1, f].astype(F32) + part_in[layer, 3, f].astype(F32),
            ):
                mean_square = jnp.mean(total * total, axis=0, keepdims=True)
                scaled.append(total * lax.rsqrt(mean_square + EPS))
            scaled = [jnp.where(mine == 0, scaled[0], scaled[1]), jnp.where(mine == 0, scaled[1], scaled[0])]
            mixed = (jnp.concatenate(scaled, axis=0).T * out_gain[pl.ds(layer, 1), :]).astype(BF16)
            if layer == 0:
                mix_buf[f, head] = mixed
                halves.append(gather_start(mix_buf.at[f], mix_send.at[f], mix_recv.at[f]))
            else:
                last_out[:, f] = mixed.reshape(NH, HROWS, 128)
        if layer == 0:
            more = [gather_forward(mix_buf.at[f], mix_send.at[f], mix_recv.at[f], halves[f]) for f in range(2)]
        else:
            copies = []
            for step in range(1, NH):
                to = (head + step) % NH
                copies.append(
                    send(last_out.at[to], last_in.at[head], last_send.at[step], last_recv.at[step], (ctx, to))
                )
            last_in[head] = last_out[head]
            gather_arrive(wout_copies, wout_more)
            before = jnp.concatenate(
                [resid[pl.ds(pl.multiple_of(f * HALF + head * HROWS, HROWS), HROWS), :] for f in range(2)], axis=0
            )
            for copy in copies:
                copy.wait_recv()
            columns = jnp.concatenate([last_in[n].reshape(ROWS, 128) for n in range(NH)], axis=1)
            delta = mm(columns, wout_buf[1].reshape(D, D))
            result[...] = (before + delta).astype(BF16)
            sent.extend(copies)
        sent.extend(exchange.values())
        for step in ZFAR:

            @pl.when((z + step) % NZ >= NEAR)
            def _(step=step):
                prior_copy(step).wait_send()

        for reach in range(1, NEAR):

            @pl.when(z < NEAR - reach)
            def _(reach=reach):
                early_copy(reach).wait_send()

        for f in range(2):
            for step in FAR:
                part_copy(step, f).wait_send()

    for copy in sent:
        copy.wait_send()


def per_device(residual, in_gain, w_in, out_gain, w_out):
    hbm = pl.BlockSpec(memory_space=pltpu.HBM)
    vmem = pl.BlockSpec(memory_space=pltpu.VMEM)
    dma = pltpu.SemaphoreType.DMA
    return pl.pallas_call(
        kernel,
        out_shape=jax.ShapeDtypeStruct((ROWS, D), BF16),
        in_specs=[hbm] * 5,
        out_specs=vmem,
        scratch_shapes=[
            pltpu.VMEM((LAYERS, D), F32),
            pltpu.VMEM((LAYERS, 128), F32),
            pltpu.VMEM((2, NH, HROWS, D), BF16),
            pltpu.VMEM((LAYERS, D, 3 * 128), BF16),
            pltpu.VMEM((LAYERS, NH, 128, D), BF16),
            pltpu.VMEM((LAYERS, 2, 2, 128, HALF), BF16),
            pltpu.VMEM((LAYERS, NY, 2, 128, HALF), BF16),
            pltpu.VMEM((LAYERS, 2, 2, HD, HALF), BF16),
            pltpu.VMEM((LAYERS, NY, 2, HD, HALF), BF16),
            pltpu.VMEM((NY, 2, HD, HALF), F32),
            pltpu.VMEM((NY, 2, HD, HALF), F32),
            pltpu.VMEM((2, SLICE, NY * TOK), BF16),
            pltpu.VMEM((2, SLICE, NY * TOK), BF16),
            pltpu.VMEM((2, SLICE, 128), F32),
            pltpu.VMEM((LAYERS, NZ, PART, 128), BF16),
            pltpu.VMEM((LAYERS, NZ, PART, 128), BF16),
            pltpu.VMEM((LAYERS, NZ, PART, 128), BF16),
            pltpu.VMEM((LAYERS, NZ, PART, 128), BF16),
            pltpu.VMEM((LAYERS, NEAR - 1, NZ, PART, 128), BF16),
            pltpu.VMEM((LAYERS, NY, 2, HD, HALF), BF16),
            pltpu.VMEM((LAYERS, NY, 2, HD, HALF), BF16),
            pltpu.VMEM((2, NH, HALF, 128), BF16),
            pltpu.VMEM((NH, 2, HROWS, 128), BF16),
            pltpu.VMEM((NH, 2, HROWS, 128), BF16),
            pltpu.VMEM((TOK, D), BF16),
            pltpu.VMEM((2 * TOK, HD), BF16),
            pltpu.VMEM((2 * TOK, HD), F32),
            pltpu.VMEM((NY, 2, HD, HALF), F32),
            pltpu.VMEM((TOK, D), F32),
            pltpu.SemaphoreType.REGULAR((3, 2)),
            dma((12,)),
            dma((2, 7)),
            dma((2, 7)),
            dma((LAYERS, 7)),
            dma((LAYERS, 7)),
            dma((LAYERS, NY, 2)),
            dma((LAYERS, NY, 2)),
            dma((LAYERS, NY)),
            dma((LAYERS, NY)),
            dma((LAYERS, NZ)),
            dma((LAYERS, NZ)),
            dma((LAYERS, NZ)),
            dma((LAYERS, NZ)),
            dma((LAYERS, NEAR - 1)),
            dma((LAYERS, NEAR - 1)),
            dma((LAYERS, NY, 2)),
            dma((LAYERS, NY, 2)),
            dma((2, 7)),
            dma((2, 7)),
            dma((NH,)),
            dma((NH,)),
        ],
        compiler_params=pltpu.CompilerParams(
            collective_id=0, has_side_effects=True, vmem_limit_bytes=40 * 1024 * 1024
        ),
        cost_estimate=pl.CostEstimate(flops=1_500_000_000, bytes_accessed=3_000_000, transcendentals=0),
    )(*[pltpu.with_memory_space_constraint(a, pltpu.HBM) for a in (residual, in_gain, w_in, out_gain, w_out)])


def solution(mesh):
    return jax.shard_map(
        per_device,
        mesh=mesh,
        in_specs=(
            P(("ctx", "head"), None),
            P(),
            P(None, None, None, "head"),
            P(None, "head"),
            P(None, "head", None),
        ),
        out_specs=P(("ctx", "head"), None),
        check_vma=False,
    )
```
